256 devices in a mesh: blk: 32 (over x_lo, z, core), sub: 8 (over x_hi, y).
Axes of the slice: x: 4 (x_hi: 2, x_lo: 2; x = x_hi * 2 + x_lo), y: 4, z: 8, core: 2. Of those that a mesh axis runs over, the one named last changes fastest.
Arguments:
- queries: bfloat16 [8, 1024, 768], P('sub', 'blk'), may hold values from -16 to 16
- codes: int32 [8, 96, 32768], P('sub', None, 'blk'), may hold values from 0 to 255
- positives: int32 [8, 1024], P('sub', 'blk'), may hold values from 0 to 32767
- codebook: bfloat16 [96, 8, 256], P('sub'), may hold values from -4 to 4
Outputs:
- query_grad: bfloat16 [8, 1024, 768], P('sub', 'blk')
- codeword_grad: float32 [96, 8, 256], P('sub')
The draws below stay inside these ranges and needn't reach their ends.
All inputs are finite; a program needn't handle non-finite values.
Results may differ from the reference program's by a relative error of at most 0.0029.
Values may be sent and summed in bfloat16 or wider, within the bound.
No kernel may reach another device: no remote copies, remote signals or barrier semaphores. Data moves between devices by JAX's collectives and lax.ppermute only.
A program may use at most 64 MiB of HBM per device.

```python
import jax
import jax.numpy as jnp
from jax import lax

MODEL_DIM = 768
SUBSPACES = 96
CODEWORDS = 256
SUB_WIDTH = 8
MICRO_BATCHES = 8
QUERY_BATCH = 1024
PASSAGE_BATCH = 32768


def shared_codes(key):
    base = jax.random.randint(jax.random.fold_in(key, 11), (MICRO_BATCHES, SUBSPACES, PASSAGE_BATCH), 0, CODEWORDS, dtype=jnp.int32)
    aligned = jnp.arange(0, QUERY_BATCH, 64)
    first = (aligned * 7 + 3) % PASSAGE_BATCH
    second = (first + PASSAGE_BATCH // 2) % PASSAGE_BATCH
    copied = base[:, 1:, first]
    return base.at[:, 1:, second].set(copied)


def shared_book(key):
    values = jnp.clip(jax.random.normal(jax.random.fold_in(key, 12), (SUBSPACES, SUB_WIDTH, CODEWORDS), jnp.float32), -4.0, 4.0)
    return values.astype(jnp.bfloat16)


def draw_codes(key, part):
    return shared_codes(key)


def draw_codebook(key, part):
    return shared_book(key)


def draw_queries(key, part):
    values = 0.09 * jnp.clip(jax.random.normal(jax.random.fold_in(key, 24), (MICRO_BATCHES, QUERY_BATCH, MODEL_DIM), jnp.float32), -6.0, 6.0)
    return values.astype(jnp.bfloat16)


def set_ends(values, own_key, smallest, high):
    spot = [jax.random.randint(jax.random.fold_in(own_key, axis), (), 0, length) for axis, length in enumerate(values.shape)]
    main_axis = values.shape.index(max(values.shape))
    next_to = spot[:main_axis] + [(spot[main_axis] + 1) % values.shape[main_axis]] + spot[main_axis + 1:]
    return values.at[tuple(spot)].set(smallest).at[tuple(next_to)].set(high)


def setup_inputs(seed: int = 0) -> dict:
    seeds = jax.random.split(jax.random.key(seed), 5)
    queries = draw_queries(jax.random.fold_in(seeds[4], 71), 0)
    codes = draw_codes(jax.random.fold_in(seeds[4], 71), 0)
    positives = set_ends(jax.random.randint(seeds[2], (MICRO_BATCHES, QUERY_BATCH), 0, PASSAGE_BATCH), jax.random.fold_in(seeds[2], 1), 0, PASSAGE_BATCH - 1).astype(jnp.int32)
    codebook = draw_codebook(jax.random.fold_in(seeds[4], 71), 0)
    return dict(queries=queries, codes=codes, positives=positives, codebook=codebook)


def decode_rows(book, code_rows):
    table = jnp.swapaxes(book, 1, 2)
    picked = table[jnp.arange(code_rows.shape[0])[:, None], code_rows]
    return jnp.transpose(picked, (1, 0, 2)).reshape(code_rows.shape[1], MODEL_DIM)


def reference(queries, codes, positives, codebook):
    def one_batch(inputs):
        query_rows, code_rows, target_rows = inputs
        passages = decode_rows(codebook, code_rows)
        scores = lax.dot_general(query_rows, passages, (((1,), (1,)), ((), ())), preferred_element_type=jnp.float32)
        peak = jnp.max(scores, axis=1)
        log_total = peak + jnp.log(jnp.sum(jnp.exp(scores - peak[:, None]), axis=1))
        hits = (target_rows[:, None] == jnp.arange(PASSAGE_BATCH, dtype=jnp.int32)[None, :]).astype(jnp.float32)
        weights = jnp.exp(scores - log_total[:, None]) - hits
        query_part = jnp.dot(weights, passages.astype(jnp.float32), precision=lax.Precision.HIGHEST, preferred_element_type=jnp.float32).astype(jnp.bfloat16)
        passage_part = lax.dot_general(weights, query_rows.astype(jnp.float32), (((0,), (0,)), ((), ())), precision=lax.Precision.HIGHEST, preferred_element_type=jnp.float32).astype(jnp.bfloat16)
        return query_part, passage_part

    query_grad, passage_grad = lax.map(one_batch, (queries, codes, positives))

    def one_subspace(index):
        columns = lax.dynamic_slice_in_dim(passage_grad, index * SUB_WIDTH, SUB_WIDTH, 2)
        columns = columns.astype(jnp.float32).reshape(MICRO_BATCHES * PASSAGE_BATCH, SUB_WIDTH)
        labels = lax.dynamic_slice_in_dim(codes, index, 1, 1).reshape(MICRO_BATCHES * PASSAGE_BATCH)
        return jax.ops.segment_sum(columns, labels, num_segments=CODEWORDS).T

    codeword_grad = lax.map(one_subspace, jnp.arange(SUBSPACES, dtype=jnp.int32))
    return query_grad, codeword_grad
```

```python
import functools

import jax
import jax.numpy as jnp
from jax import lax
from jax.experimental import pallas as pl
from jax.experimental.pallas import tpu as pltpu
from jax.sharding import Mesh, PartitionSpec as P

f32 = jnp.float32
bf16 = jnp.bfloat16
LANES = 128


def decode_kernel(codes_ref, book_ref, out_ref):
    def pair(j, carry):
        rows = []
        for h in range(2):
            m = 2 * j + h
            table = book_ref[m].astype(f32)
            low, high = table[:, :LANES], table[:, LANES:]
            row = codes_ref[pl.ds(m, 1), :]
            parts = []
            for t in range(row.shape[1] // LANES):
                code = jnp.broadcast_to(row[:, t * LANES : (t + 1) * LANES], (8, LANES))
                index = code & (LANES - 1)
                parts.append(
                    jnp.where(
                        code < LANES,
                        jnp.take_along_axis(low, index, axis=1, mode="promise_in_bounds"),
                        jnp.take_along_axis(high, index, axis=1, mode="promise_in_bounds"),
                    )
                )
            rows.append(jnp.concatenate(parts, axis=1))
        out_ref[pl.ds(pl.multiple_of(16 * j, 16), 16), :] = jnp.concatenate(rows, axis=0).astype(bf16)
        return carry

    lax.fori_loop(0, codes_ref.shape[0] // 2, pair, 0, unroll=4)


def as_row(column):
    return jnp.transpose(jnp.broadcast_to(column, (column.shape[0], LANES)))[:1]


def as_column(row):
    return jnp.transpose(jnp.broadcast_to(row, (LANES, row.shape[1])))[:, :1]


def scores_kernel(own_ref, other_ref, passages_ref, positives_ref, scores_ref, stats_ref):
    half = own_ref.shape[0]
    peers = stats_ref.shape[0]
    block = 256
    for b in range(2 * half // block):
        source = own_ref if b * block < half else other_ref
        start = b * block % half
        tile = jnp.dot(source[start : start + block], passages_ref[...], preferred_element_type=f32)
        scores_ref[b * block : (b + 1) * block] = tile
        peak = jnp.max(tile, axis=1, keepdims=True)
        total = jnp.sum(jnp.exp(tile - peak), axis=1, keepdims=True)
        row = as_row(peak + jnp.log(total))
        stats_ref[:, b * block : (b + 1) * block] = jnp.broadcast_to(row, (peers, block))
    stats_ref[:, 2 * half :] = jnp.broadcast_to(positives_ref[...], (peers, LANES))


def transpose_kernel(own_ref, other_ref, out_ref):
    half = own_ref.shape[0]
    out_ref[:, :half] = jnp.transpose(own_ref[...])
    out_ref[:, half:] = jnp.transpose(other_ref[...])


def weights_kernel(
    place_ref, scores_ref, stats_ref, turned_ref, codes_ref, high_ref, low_ref, sums_ref, grads_ref
):
    core, offset = place_ref[0], place_ref[1]
    query_count, passage_count = scores_ref.shape
    half = query_count // 2
    peers = stats_ref.shape[0]
    chips = peers // 2
    size = half // chips
    first, second = stats_ref[:, :half], stats_ref[:, half : 2 * half]
    same = (lax.broadcasted_iota(jnp.int32, (peers, half), 0) & 1) == core
    targets = jnp.concatenate([stats_ref[:, 2 * half :], jnp.zeros((LANES - peers, LANES), f32)], axis=0)
    targets = jnp.transpose(targets)[:size].astype(jnp.int32)
    spot = lax.broadcasted_iota(jnp.int32, (size, passage_count), 1) + offset
    for h in range(2):
        logs = jnp.where(same, first, second) if h == 0 else jnp.where(same, second, first)
        peak = jnp.max(logs, axis=0, keepdims=True)
        log_total = as_column(peak + jnp.log(jnp.sum(jnp.exp(logs - peak), axis=0, keepdims=True)))
        for c in range(chips):
            rows = slice(h * half + c * size, h * half + (c + 1) * size)
            target = jnp.where(core == h, targets[:, 2 * c : 2 * c + 1], targets[:, 2 * c + 1 : 2 * c + 2])
            weight = jnp.exp(scores_ref[rows] - log_total[c * size : (c + 1) * size])
            weight = weight - jnp.where(target == spot, 1.0, 0.0)
            high = weight.astype(bf16)
            high_ref[rows] = high
            low_ref[rows] = (weight - high.astype(f32)).astype(bf16)
    block = 256
    for b in range(turned_ref.shape[0] // block):
        part = turned_ref[b * block : (b + 1) * block]
        grads_ref[b * block : (b + 1) * block] = jnp.dot(
            part, high_ref[...], preferred_element_type=f32
        ) + jnp.dot(part, low_ref[...], preferred_element_type=f32)

    word = lax.broadcasted_iota(jnp.int32, (LANES, passage_count), 0)

    def subspace(m, carry):
        grad = grads_ref[pl.ds(pl.multiple_of(8 * m, 8), 8), :]
        code = codes_ref[pl.ds(m, 1), :]
        split = code < LANES
        both = jnp.concatenate([jnp.where(split, grad, 0.0), jnp.where(split, 0.0, grad)], axis=0).astype(bf16)
        onehot = jnp.where((code & (LANES - 1)) == word, 1.0, 0.0).astype(bf16)
        sums = lax.dot_general(both, onehot, (((1,), (1,)), ((), ())), preferred_element_type=f32)
        sums_ref[m, :, :LANES] = sums[:8]
        sums_ref[m, :, LANES:] = sums[8:]
        return carry

    lax.fori_loop(0, codes_ref.shape[0], subspace, 0, unroll=2)


def query_kernel(high_ref, low_ref, passages_ref, own_ref, other_ref):
    half = own_ref.shape[0]
    block = 256
    dims = (((1,), (1,)), ((), ()))
    for b in range(2 * half // block):
        rows = slice(b * block, (b + 1) * block)
        part = lax.dot_general(
            high_ref[rows], passages_ref[...], dims, preferred_element_type=f32
        ) + lax.dot_general(low_ref[rows], passages_ref[...], dims, preferred_element_type=f32)
        start = b * block % half
        if b * block < half:
            own_ref[start : start + block] = part
        else:
            other_ref[start : start + block] = part


def call(kernel, shapes, args, flops, scratch=(), scalars=False, vmem=40):
    specs = [pl.BlockSpec(memory_space=pltpu.VMEM)] * len(args)
    if scalars:
        specs[0] = pl.BlockSpec(memory_space=pltpu.SMEM)
    many = isinstance(shapes, list)
    return pl.pallas_call(
        kernel,
        out_shape=shapes,
        in_specs=specs,
        out_specs=[pl.BlockSpec(memory_space=pltpu.VMEM)] * len(shapes) if many else pl.BlockSpec(memory_space=pltpu.VMEM),
        scratch_shapes=scratch,
        compiler_params=pltpu.CompilerParams(vmem_limit_bytes=vmem * 2**20),
        cost_estimate=pl.CostEstimate(flops=flops, bytes_accessed=4 * 2**20, transcendentals=0),
    )(*args)


CHIP = ("xl", "z")
SUB = ("xh", "y")


def spread(value, axes):
    peers = lax.axis_size(axes)
    copies = jnp.broadcast_to(value[None], (peers, *value.shape))
    return lax.all_to_all(copies, axes, 0, 0)


def per_device(queries, codes, positives, codebook):
    swap = functools.partial(lax.ppermute, axis_name="core", perm=[(0, 1), (1, 0)])
    shape = jax.ShapeDtypeStruct
    own_codes = codes[0]
    subspaces, passage_count = own_codes.shape
    width = queries.shape[2]
    core = lax.axis_index("core")
    offset = lax.axis_index(("xl", "z", "core")) * passage_count
    place = jnp.stack([core, offset]).astype(jnp.int32)
    book = spread(codebook, SUB).reshape(subspaces, *codebook.shape[1:])
    own = spread(queries[0], CHIP).reshape(-1, width)
    passages = call(decode_kernel, shape((width, passage_count), bf16), (own_codes, book), 10**9)
    other = swap(own)
    half = own.shape[0]
    targets = jnp.pad(positives.astype(f32), ((0, 0), (0, LANES - positives.shape[1])))
    scores, stats = call(
        scores_kernel,
        [shape((2 * half, passage_count), f32), shape((32, 2 * half + LANES), f32)],
        (own, other, passages, targets),
        2 * 10**9,
    )
    stats = lax.all_to_all(stats, CHIP + ("core",), 0, 0, tiled=True)
    turned = call(transpose_kernel, shape((width, 2 * half), bf16), (own, other), 10**9)
    high, low, sums = call(
        weights_kernel,
        [
            shape((2 * half, passage_count), bf16),
            shape((2 * half, passage_count), bf16),
            shape((subspaces, 8, 256), f32),
        ],
        (place, scores, stats, turned, own_codes),
        8 * 10**9,
        scratch=[pltpu.VMEM((width, passage_count), f32)],
        scalars=True,
    )
    parts = sums.reshape(8, 2, subspaces // 16, 8, 256)
    parts = jnp.swapaxes(parts, 0, 1).reshape(16, subspaces // 16, 8, 256)
    parts = jnp.sum(lax.all_to_all(parts, ("core",) + SUB, 0, 0), axis=0)
    query_own, query_other = call(
        query_kernel,
        [shape((half, width), f32), shape((half, width), f32)],
        (high, low, passages),
        4 * 10**9,
    )
    query_sums = query_own + swap(query_other)
    query_sums = lax.all_to_all(query_sums.reshape(16, half // 16, width), CHIP, 0, 0)
    query_grad = jnp.sum(query_sums, axis=0).astype(bf16)
    parts = jnp.sum(spread(parts, CHIP), axis=0)
    cross = swap(parts)
    codeword_grad = jnp.concatenate(
        [jnp.where(core == 0, parts, cross), jnp.where(core == 0, cross, parts)], axis=0
    )
    return query_grad[None], codeword_grad


def solution(mesh):
    split = Mesh(mesh.devices.reshape(2, 8, 2, 2, 4), ("xl", "z", "core", "xh", "y"))
    blk = ("xl", "z", "core")
    return jax.shard_map(
        per_device,
        mesh=split,
        in_specs=(P(SUB, blk, None), P(SUB, None, blk), P(SUB, blk), P(SUB, None, None)),
        out_specs=(P(SUB, blk, None), P(SUB, None, None)),
        check_vma=False,
    )
```

```python
import functools

import jax
import jax.numpy as jnp
from jax import lax
from jax.experimental import pallas as pl
from jax.experimental.pallas import tpu as pltpu
from jax.sharding import Mesh, PartitionSpec as P

f32 = jnp.float32
bf16 = jnp.bfloat16
i32 = jnp.int32
i16 = jnp.int16
LANES = 128
BLOCK = 256
CHIP = ("xl", "z")
SUB = ("xh", "y")
ROWS_BY_ROWS = (((1,), (1,)), ((), ()))


def as_column(row):
    return jnp.transpose(jnp.broadcast_to(row, (LANES, row.shape[1])))[:, :1]


def as_row(column):
    return jnp.transpose(jnp.broadcast_to(column, (column.shape[0], LANES)))[:1]


def exponents(rows):
    peak = jnp.maximum(jnp.max(jnp.abs(rows), axis=1, keepdims=True), 2.0**-100)
    return jnp.ceil(jnp.log2(peak * (1.0 / 32767.0)))


def as_words(rows, exponent):
    scaled = jnp.round(rows * jnp.exp2(-exponent))
    return jnp.clip(scaled, -32767.0, 32767.0).astype(i32).astype(i16)


def exponent_rows(exponent):
    column = jnp.concatenate([exponent, jnp.zeros((LANES - exponent.shape[0], 1), f32)], axis=0)
    return jnp.transpose(jnp.broadcast_to(column, (LANES, LANES)))[:16].astype(i32).astype(i16)


def scale_column(rows, count):
    row = rows.astype(i32).astype(f32)[:1]
    return jnp.exp2(jnp.transpose(jnp.broadcast_to(row, (LANES, LANES)))[:count])


def spread_kernel(queries_ref, positives_ref, out_ref):
    size, width = queries_ref.shape
    target = positives_ref[...]
    tail = jnp.concatenate([target // LANES, target % LANES, jnp.zeros((14, LANES), i32)], axis=0)
    tail = tail.astype(f32).astype(bf16)
    for c in range(out_ref.shape[0]):
        for t in range(width // LANES):
            out_ref[c, t * size : (t + 1) * size] = queries_ref[:, t * LANES : (t + 1) * LANES]
        out_ref[c, width // LANES * size :] = tail


def query_columns(pack_ref, t, first, count):
    size = (pack_ref.shape[1] - 16) // 6
    return pack_ref[first : first + count, t * size : (t + 1) * size, :].reshape(count * size, LANES)


def query_rows(pack_ref, first, count):
    return jnp.concatenate([query_columns(pack_ref, t, first, count) for t in range(6)], axis=1)


def target_columns(pack_ref):
    chips, length, _ = pack_ref.shape
    tail = pack_ref[:, length - 16 :, :].astype(f32)
    target = tail[:, 0, :] * LANES + tail[:, 1, :]
    target = jnp.concatenate([target, jnp.zeros((LANES - chips, LANES), f32)], axis=0)
    return jnp.transpose(target)


def decode_kernel(place_ref, codes_ref, near_ref, far_ref, out_ref):
    share = near_ref.shape[1]
    far, along = place_ref[2], place_ref[3]

    def table_of(group, member):
        piece = (along + 4 - group % 4) % 4
        near, other = near_ref[piece, member], far_ref[piece, member]
        return jnp.where(group // 4 == far, near, other).astype(f32)

    for group in range(8):

        def pair(j, carry, group=group):
            rows = []
            for h in range(2):
                table = table_of(group, 2 * j + h)
                low, high = table[:, :LANES], table[:, LANES:]
                row = codes_ref[pl.ds(group * share + 2 * j + h, 1), :]
                parts = []
                for t in range(row.shape[1] // LANES):
                    code = jnp.broadcast_to(row[:, t * LANES : (t + 1) * LANES], (8, LANES))
                    index = code & (LANES - 1)
                    parts.append(
                        jnp.where(
                            code < LANES,
                            jnp.take_along_axis(low, index, axis=1, mode="promise_in_bounds"),
                            jnp.take_along_axis(high, index, axis=1, mode="promise_in_bounds"),
                        )
                    )
                rows.append(jnp.concatenate(parts, axis=1))
            start = pl.multiple_of(16 * (group * share // 2 + j), 16)
            out_ref[pl.ds(start, 16), :] = jnp.concatenate(rows, axis=0).astype(bf16)
            return carry

        lax.fori_loop(0, share // 2, pair, 0, unroll=2)


def scores_kernel(own_ref, other_ref, passages_ref, stats_ref):
    for b in range(4):
        rows = query_rows(own_ref if b < 2 else other_ref, b % 2 * 8, 8)
        tile = jnp.dot(rows, passages_ref[...], preferred_element_type=f32)
        peak = jnp.max(tile, axis=1, keepdims=True)
        total = jnp.sum(jnp.exp(tile - peak), axis=1, keepdims=True)
        row = as_row(peak + jnp.log(total))
        for j in range(2):
            piece = row[:, j * LANES : (j + 1) * LANES]
            stats_ref[:, 2 * b + j : 2 * b + j + 1, :] = jnp.broadcast_to(piece[None], (stats_ref.shape[0], 1, LANES))


def log_totals(core, stats_ref, h):
    peers = stats_ref.shape[0]
    same = (lax.broadcasted_iota(i32, (peers, LANES), 0) & 1) == core
    out = []
    for j in range(4):
        logs = jnp.where(same, stats_ref[:, 4 * h + j, :], stats_ref[:, 4 - 4 * h + j, :])
        peak = jnp.max(logs, axis=0, keepdims=True)
        out.append(peak + jnp.log(jnp.sum(jnp.exp(logs - peak), axis=0, keepdims=True)))
    return out


def weights_kernel(
    place_ref, stats_ref, own_ref, other_ref, passages_ref, other_sums_ref, own_sums_ref, grads_ref, high_ref, low_ref
):
    core, offset = place_ref[0], place_ref[1]
    half, passage_count = own_sums_ref.shape[0], passages_ref.shape[1]
    size = half // own_ref.shape[0]
    passages = passages_ref[...]
    spot = lax.broadcasted_iota(i32, (size, passage_count), 1) + offset
    for h, pack_ref, sums_ref in ((1, other_ref, other_sums_ref), (0, own_ref, own_sums_ref)):
        totals = [as_column(row) for row in log_totals(core, stats_ref, h)]
        targets = target_columns(pack_ref)[:size].astype(i32)
        for b in range(half // BLOCK):
            tile = jnp.dot(query_rows(pack_ref, b * 8, 8), passages, preferred_element_type=f32)
            tile = jnp.exp(tile - jnp.concatenate(totals[2 * b : 2 * b + 2], axis=0))
            rows = slice(h * half + b * BLOCK, h * half + (b + 1) * BLOCK)
            pieces = []
            for c in range(BLOCK // size):
                place = b * BLOCK // size + c
                hits = jnp.where(targets[:, place : place + 1] == spot, 1.0, 0.0)
                pieces.append(tile[c * size : (c + 1) * size] - hits)
            weight = jnp.concatenate(pieces, axis=0)
            high = weight.astype(bf16)
            low = (weight - high.astype(f32)).astype(bf16)
            high_ref[rows] = high
            low_ref[rows] = low
            sums_ref[b * BLOCK : (b + 1) * BLOCK] = lax.dot_general(
                high, passages, ROWS_BY_ROWS, preferred_element_type=f32
            ) + lax.dot_general(low, passages, ROWS_BY_ROWS, preferred_element_type=f32)
    chips = own_ref.shape[0]
    for t in range(3):
        turned = jnp.concatenate(
            [
                jnp.concatenate(
                    [jnp.transpose(query_columns(pack_ref, 2 * t + k, 0, chips)) for pack_ref in (own_ref, other_ref)],
                    axis=1,
                )
                for k in range(2)
            ],
            axis=0,
        )
        grad = jnp.dot(turned, high_ref[...], preferred_element_type=f32) + jnp.dot(
            turned, low_ref[...], preferred_element_type=f32
        )
        grads_ref[t * BLOCK : (t + 1) * BLOCK] = grad.astype(bf16)


def codeword_kernel(mine, place_ref, grads_ref, codes_ref, out_ref):
    core = place_ref[0] if mine else 1 - place_ref[0]
    word = lax.broadcasted_iota(i32, (32, codes_ref.shape[1]), 0)

    def four(j, carry):
        sums = []
        for m in range(4):
            grad = grads_ref[pl.ds(pl.multiple_of(32 * j + 16 * (m // 2), 16), 16), :].astype(f32)
            grad = grad[m % 2 * 8 : m % 2 * 8 + 8]
            code = codes_ref[pl.ds(4 * j + m, 1), :]
            high = (code >> 5) - 4 * core
            parts = jnp.concatenate([jnp.where(high == t, grad, 0.0) for t in range(4)], axis=0).astype(bf16)
            onehot = jnp.where((code & 31) == word, 1.0, 0.0).astype(bf16)
            sums.append(lax.dot_general(parts, onehot, ROWS_BY_ROWS, preferred_element_type=f32))
        sums = jnp.concatenate(sums, axis=1)
        for k in range(2):
            out_ref[j // 3, k, j % 3] = sums[16 * k : 16 * k + 16]
        return carry

    lax.fori_loop(0, codes_ref.shape[0] // 4, four, 0, unroll=4)


def put_query_words(chunk, out_ref, c):
    size, width = chunk.shape
    exponent = exponents(chunk)
    words = as_words(chunk, exponent)
    for t in range(width // LANES):
        out_ref[c, t * size : (t + 1) * size] = words[:, t * LANES : (t + 1) * LANES]
    return exponent


def take_query_words(words_ref, c, scale, width):
    size = scale.shape[0]
    words = [words_ref[c, t * size : (t + 1) * size] for t in range(width // LANES)]
    return jnp.concatenate([word.astype(i32).astype(f32) * scale for word in words], axis=1)


def send_kernel(place_ref, sums_ref, cross_ref, out_ref):
    peers = out_ref.shape[0]
    half, width = sums_ref.shape
    size = half // (2 * peers)
    for c in range(peers):
        rows = pl.ds(pl.multiple_of((1 - place_ref[4]) * (half // 2) + c * size, size), size)
        exponent = put_query_words(sums_ref[rows] + cross_ref[rows], out_ref, c)
        out_ref[c, width // LANES * size :] = exponent_rows(exponent)


def pack_kernel(place_ref, sums_ref, cross_ref, words_ref, parts_ref, out_ref):
    peers = out_ref.shape[0]
    half, width = sums_ref.shape
    size = half // (2 * peers)
    base = width // LANES * size
    totals = parts_ref[0]
    for c in range(1, parts_ref.shape[0]):
        totals = totals + parts_ref[c]
    totals = totals.reshape(-1, LANES)
    totals_exponent = exponents(totals)
    totals = as_words(totals, totals_exponent)
    for c in range(peers):
        rows = pl.ds(pl.multiple_of(place_ref[4] * (half // 2) + c * size, size), size)
        received = take_query_words(words_ref, c, scale_column(words_ref[c, base:], size), width)
        exponent = put_query_words(sums_ref[rows] + cross_ref[rows] + received, out_ref, c)
        out_ref[c, base : base + totals.shape[0]] = totals
        out_ref[c, base + totals.shape[0] :] = exponent_rows(jnp.concatenate([exponent, totals_exponent], axis=0))


def unpack_kernel(words_ref, query_ref, sums_ref):
    peers = words_ref.shape[0]
    size, width = query_ref.shape
    base = width // LANES * size
    count = sums_ref.shape[0]
    query, sums = 0.0, 0.0
    for c in range(peers):
        scale = scale_column(words_ref[c, base + count :], size + count)
        query = query + take_query_words(words_ref, c, scale[:size], width)
        sums = sums + words_ref[c, base : base + count].astype(i32).astype(f32) * scale[size:]
    query_ref[...] = query.astype(bf16)
    sums_ref[...] = sums


def join_kernel(place_ref, own_ref, beside_ref, cross_ref, out_ref, all_ref):
    core, side = place_ref[0], place_ref[4]
    count = own_ref.shape[0]
    all_ref[2 * core + side] = own_ref[...]
    all_ref[2 * core + 1 - side] = beside_ref[...]
    all_ref[2 - 2 * core + side] = cross_ref[:count]
    all_ref[2 - 2 * core + 1 - side] = cross_ref[count:]
    for j in range(3):
        rows = [all_ref[t // 2, 16 * j + t % 2 * 8 : 16 * j + t % 2 * 8 + 8] for t in range(8)]
        for m in range(4):
            out_ref[4 * j + m] = jnp.concatenate([row[:, 32 * m : 32 * m + 32] for row in rows], axis=1)


IN_VMEM = pl.BlockSpec(memory_space=pltpu.VMEM)
IN_SMEM = pl.BlockSpec(memory_space=pltpu.SMEM)


def call(kernel, shapes, args, flops, scratch=(), special=None, out_special=None, vmem=12):
    specs = [IN_VMEM] * len(args)
    for place, spec in (special or {}).items():
        specs[place] = spec
    many = isinstance(shapes, list)
    outs = [IN_VMEM] * (len(shapes) if many else 1)
    for place, spec in (out_special or {}).items():
        outs[place] = spec
    return pl.pallas_call(
        kernel,
        out_shape=shapes,
        in_specs=specs,
        out_specs=outs if many else outs[0],
        scratch_shapes=scratch,
        compiler_params=pltpu.CompilerParams(vmem_limit_bytes=vmem * 2**20),
        cost_estimate=pl.CostEstimate(flops=flops, bytes_accessed=2**16, transcendentals=0),
    )(*args)


def per_device(queries, codes, positives, codebook):
    swap = functools.partial(lax.ppermute, axis_name="core", perm=[(0, 1), (1, 0)])
    swap_x = functools.partial(lax.ppermute, axis_name="xl", perm=[(0, 1), (1, 0)])
    shape = jax.ShapeDtypeStruct
    own_codes = codes[0]
    subspaces, passage_count = own_codes.shape
    size, width = queries.shape[1:]
    chips = 16
    half = chips * size
    offset = lax.axis_index(("xl", "z", "core")) * passage_count
    axes = [lax.axis_index(name) for name in ("core", "xh", "y", "xl")]
    place = jnp.stack([axes[0], offset, *axes[1:]]).astype(i32)
    scalar = {0: IN_SMEM}
    length = width // LANES * size + 16
    near = [codebook] + [lax.ppermute(codebook, "y", [(i, (i + k) % 4) for i in range(4)]) for k in range(1, 4)]
    near = jnp.stack(near)
    far = lax.ppermute(near, "xh", [(0, 1), (1, 0)])
    targets = jnp.pad(positives, ((0, 0), (0, LANES - size)))
    own = call(spread_kernel, shape((chips, length, LANES), bf16), (queries[0], targets), 10**6)
    own = lax.all_to_all(own, CHIP, 0, 0)
    passages = call(
        decode_kernel, shape((width, passage_count), bf16), (place, own_codes, near, far), 10**6, special=scalar
    )
    own, passages = lax.optimization_barrier((own, passages))
    other = swap(own)
    stats = call(scores_kernel, shape((32, 8, LANES), f32), (own, other, passages), 10**6)
    stats = lax.all_to_all(stats, CHIP + ("core",), 0, 0, tiled=True)
    query_other, query_own, grads = call(
        weights_kernel,
        [shape((half, width), f32), shape((half, width), f32), shape((width, passage_count), bf16)],
        (place, stats, own, other, passages),
        10**6,
        scratch=[pltpu.VMEM((2 * half, passage_count), bf16), pltpu.VMEM((2 * half, passage_count), bf16)],
        special=scalar,
        vmem=20,
    )
    query_cross = swap(query_other)

    def codeword_sums(mine):
        return call(
            functools.partial(codeword_kernel, mine),
            shape((8, 2, subspaces // 32, 16, LANES), f32),
            (place, grads, own_codes),
            10**6,
            special=scalar,
        )

    sums_cross = swap(codeword_sums(False))
    parts = codeword_sums(True) + sums_cross
    words = call(
        send_kernel, shape((chips // 2, length, LANES), i16), (place, query_own, query_cross), 10**6, special=scalar
    )
    parts, words = lax.optimization_barrier((parts, words))
    words = swap_x(words)
    parts = lax.all_to_all(parts.reshape(16, subspaces // 32, 16, LANES), SUB + ("xl",), 0, 0)
    count = subspaces // 32 * 16
    words = call(
        pack_kernel,
        shape((chips // 2, length + count, LANES), i16),
        (place, query_own, query_cross, words, parts),
        10**6,
        special=scalar,
    )
    words = lax.all_to_all(words, "z", 0, 0)
    query_grad, sums = call(unpack_kernel, [shape((size, width), bf16), shape((count, LANES), f32)], (words,), 10**6)
    beside = swap_x(sums)
    cross = swap(jnp.concatenate([sums, beside]))
    codeword_grad = call(
        join_kernel,
        shape((subspaces // 8, 8, 2 * LANES), f32),
        (place, sums, beside, cross),
        10**6,
        scratch=[pltpu.VMEM((4, count, LANES), f32)],
        special=scalar,
    )
    return query_grad[None], codeword_grad


def solution(mesh):
    split = Mesh(mesh.devices.reshape(2, 8, 2, 2, 4), ("xl", "z", "core", "xh", "y"))
    blk = ("xl", "z", "core")
    return jax.shard_map(
        per_device,
        mesh=split,
        in_specs=(P(SUB, blk, None), P(SUB, None, blk), P(SUB, blk), P(SUB, None, None)),
        out_specs=(P(SUB, blk, None), P(SUB, None, None)),
        check_vma=False,
    )
```

```python
import functools

import jax
import jax.numpy as jnp
from jax import lax
from jax.experimental import pallas as pl
from jax.experimental.pallas import tpu as pltpu
from jax.sharding import Mesh, PartitionSpec as P

f32 = jnp.float32
bf16 = jnp.bfloat16
i32 = jnp.int32
i16 = jnp.int16
LANES = 128
BLOCK = 256
CHIP = ("xl", "z")
SUB = ("xh", "y")
ROWS_BY_ROWS = (((1,), (1,)), ((), ()))


def as_column(row):
    return jnp.transpose(jnp.broadcast_to(row, (LANES, row.shape[1])))[:, :1]


def as_row(column):
    return jnp.transpose(jnp.broadcast_to(column, (column.shape[0], LANES)))[:1]


def exponents(rows):
    peak = jnp.maximum(jnp.max(jnp.abs(rows), axis=1, keepdims=True), 2.0**-100)
    return jnp.ceil(jnp.log2(peak * (1.0 / 32767.0)))


def as_words(rows, exponent):
    scaled = jnp.round(rows * jnp.exp2(-exponent))
    return jnp.clip(scaled, -32767.0, 32767.0).astype(i32).astype(i16)


def exponent_rows(exponent):
    column = jnp.concatenate([exponent, jnp.zeros((LANES - exponent.shape[0], 1), f32)], axis=0)
    return jnp.transpose(jnp.broadcast_to(column, (LANES, LANES)))[:16].astype(i32).astype(i16)


def scale_column(rows, count):
    row = rows.astype(i32).astype(f32)[:1]
    return jnp.exp2(jnp.transpose(jnp.broadcast_to(row, (LANES, LANES)))[:count])


def spread_kernel(place_ref, queries_ref, positives_ref, book_ref, out_ref, share_ref):
    size, width = queries_ref.shape
    target = jnp.concatenate([positives_ref[...], jnp.zeros((1, LANES - size), i32)], axis=1)
    tail = jnp.concatenate([target // LANES, target % LANES, jnp.zeros((14, LANES), i32)], axis=0)
    tail = tail.astype(f32).astype(bf16)
    for c in range(out_ref.shape[0]):
        for t in range(width // LANES):
            out_ref[c, t * size : (t + 1) * size] = queries_ref[:, t * LANES : (t + 1) * LANES]
        out_ref[c, width // LANES * size :] = tail
    count = share_ref.shape[0]
    share_ref[...] = book_ref[pl.ds(place_ref[0] * count, count)]


def query_columns(pack_ref, t, first, count):
    size = (pack_ref.shape[1] - 16) // 6
    return pack_ref[first : first + count, t * size : (t + 1) * size, :].reshape(count * size, LANES)


def query_rows(pack_ref, first, count):
    return jnp.concatenate([query_columns(pack_ref, t, first, count) for t in range(6)], axis=1)


def target_columns(pack_ref):
    chips, length, _ = pack_ref.shape
    tail = pack_ref[:, length - 16 :, :].astype(f32)
    target = tail[:, 0, :] * LANES + tail[:, 1, :]
    target = jnp.concatenate([target, jnp.zeros((LANES - chips, LANES), f32)], axis=0)
    return jnp.transpose(target)


def decode_kernel(place_ref, codes_ref, near_ref, near_cross_ref, far_ref, far_cross_ref, out_ref):
    core, far_side, along = place_ref[0], 1 - place_ref[2], place_ref[3]
    share = near_ref.shape[1]

    def pair(j, carry):
        side, group, c, k = j // (4 * share), j // share % 4, j // (share // 2) % 2, j % (share // 2) * 2
        piece = (along + 4 - group) % 4
        rows = []
        for h in range(2):
            near = jnp.where(core == c, near_ref[piece, k + h].astype(f32), near_cross_ref[piece, k + h].astype(f32))
            far = jnp.where(core == c, far_ref[piece, k + h].astype(f32), far_cross_ref[piece, k + h].astype(f32))
            table = jnp.where(side == far_side, far, near)
            low, high = table[:, :LANES], table[:, LANES:]
            row = codes_ref[pl.ds(2 * j + h, 1), :]
            parts = []
            for t in range(row.shape[1] // LANES):
                code = jnp.broadcast_to(row[:, t * LANES : (t + 1) * LANES], (8, LANES))
                index = code & (LANES - 1)
                parts.append(
                    jnp.where(
                        code < LANES,
                        jnp.take_along_axis(low, index, axis=1, mode="promise_in_bounds"),
                        jnp.take_along_axis(high, index, axis=1, mode="promise_in_bounds"),
                    )
                )
            rows.append(jnp.concatenate(parts, axis=1))
        out_ref[pl.ds(pl.multiple_of(16 * j, 16), 16), :] = jnp.concatenate(rows, axis=0).astype(bf16)
        return carry

    lax.fori_loop(0, codes_ref.shape[0] // 2, pair, 0, unroll=8)


def scores_kernel(own_ref, other_ref, passages_ref, stats_ref):
    for b in range(4):
        rows = query_rows(own_ref if b < 2 else other_ref, b % 2 * 8, 8)
        tile = jnp.dot(rows, passages_ref[...], preferred_element_type=f32)
        peak = jnp.max(tile, axis=1, keepdims=True)
        total = jnp.sum(jnp.exp(tile - peak), axis=1, keepdims=True)
        row = as_row(peak + jnp.log(total))
        for j in range(2):
            piece = row[:, j * LANES : (j + 1) * LANES]
            stats_ref[:, 2 * b + j : 2 * b + j + 1, :] = jnp.broadcast_to(piece[None], (stats_ref.shape[0], 1, LANES))


def log_totals(core, stats_ref, h):
    peers = stats_ref.shape[0]
    same = (lax.broadcasted_iota(i32, (peers, LANES), 0) & 1) == core
    out = []
    for j in range(4):
        logs = jnp.where(same, stats_ref[:, 4 * h + j, :], stats_ref[:, 4 - 4 * h + j, :])
        peak = jnp.max(logs, axis=0, keepdims=True)
        out.append(peak + jnp.log(jnp.sum(jnp.exp(logs - peak), axis=0, keepdims=True)))
    return out


def weights_kernel(
    place_ref, stats_ref, own_ref, other_ref, passages_ref, other_sums_ref, own_sums_ref, grads_ref, high_ref, low_ref
):
    core, offset = place_ref[0], place_ref[1]
    half, passage_count = own_sums_ref.shape[0], passages_ref.shape[1]
    size = half // own_ref.shape[0]
    passages = passages_ref[...]
    spot = lax.broadcasted_iota(i32, (size, passage_count), 1) + offset
    for h, pack_ref, sums_ref in ((1, other_ref, other_sums_ref), (0, own_ref, own_sums_ref)):
        totals = [as_column(row) for row in log_totals(core, stats_ref, h)]
        targets = target_columns(pack_ref)[:size].astype(i32)
        for b in range(half // BLOCK):
            tile = jnp.dot(query_rows(pack_ref, b * 8, 8), passages, preferred_element_type=f32)
            tile = jnp.exp(tile - jnp.concatenate(totals[2 * b : 2 * b + 2], axis=0))
            rows = slice(h * half + b * BLOCK, h * half + (b + 1) * BLOCK)
            pieces = []
            for c in range(BLOCK // size):
                place = b * BLOCK // size + c
                hits = jnp.where(targets[:, place : place + 1] == spot, 1.0, 0.0)
                pieces.append(tile[c * size : (c + 1) * size] - hits)
            weight = jnp.concatenate(pieces, axis=0)
            high = weight.astype(bf16)
            low = (weight - high.astype(f32)).astype(bf16)
            high_ref[rows] = high
            low_ref[rows] = low
            sums_ref[b * BLOCK : (b + 1) * BLOCK] = lax.dot_general(
                high, passages, ROWS_BY_ROWS, preferred_element_type=f32
            ) + lax.dot_general(low, passages, ROWS_BY_ROWS, preferred_element_type=f32)
    chips = own_ref.shape[0]
    for t in range(3):
        turned = jnp.concatenate(
            [
                jnp.concatenate(
                    [jnp.transpose(query_columns(pack_ref, 2 * t + k, 0, chips)) for pack_ref in (own_ref, other_ref)],
                    axis=1,
                )
                for k in range(2)
            ],
            axis=0,
        )
        grad = jnp.dot(turned, high_ref[...], preferred_element_type=f32) + jnp.dot(
            turned, low_ref[...], preferred_element_type=f32
        )
        grads_ref[t * BLOCK : (t + 1) * BLOCK] = grad.astype(bf16)


def codeword_kernel(mine, place_ref, grads_ref, codes_ref, out_ref):
    core = place_ref[0] if mine else 1 - place_ref[0]
    word = lax.broadcasted_iota(i32, (32, codes_ref.shape[1]), 0)

    def four(j, carry):
        sums = []
        for m in range(4):
            grad = grads_ref[pl.ds(pl.multiple_of(32 * j + 16 * (m // 2), 16), 16), :].astype(f32)
            grad = grad[m % 2 * 8 : m % 2 * 8 + 8]
            code = codes_ref[pl.ds(4 * j + m, 1), :]
            high = (code >> 5) - 4 * core
            parts = jnp.concatenate([jnp.where(high == t, grad, 0.0) for t in range(4)], axis=0).astype(bf16)
            onehot = jnp.where((code & 31) == word, 1.0, 0.0).astype(bf16)
            sums.append(lax.dot_general(parts, onehot, ROWS_BY_ROWS, preferred_element_type=f32))
        sums = jnp.concatenate(sums, axis=1)
        for k in range(2):
            out_ref[j // 3, k, j % 3] = sums[16 * k : 16 * k + 16]
        return carry

    lax.fori_loop(0, codes_ref.shape[0] // 4, four, 0, unroll=8)


def put_query_words(chunk, out_ref, c):
    size, width = chunk.shape
    exponent = exponents(chunk)
    words = as_words(chunk, exponent)
    for t in range(width // LANES):
        out_ref[c, t * size : (t + 1) * size] = words[:, t * LANES : (t + 1) * LANES]
    return exponent


def take_query_words(words_ref, c, scale, width):
    size = scale.shape[0]
    words = [words_ref[c, t * size : (t + 1) * size] for t in range(width // LANES)]
    return jnp.concatenate([word.astype(i32).astype(f32) * scale for word in words], axis=1)


def send_kernel(place_ref, sums_ref, cross_ref, out_ref):
    peers = out_ref.shape[0]
    half, width = sums_ref.shape
    size = half // (2 * peers)
    for c in range(peers):
        rows = pl.ds(pl.multiple_of((1 - place_ref[4]) * (half // 2) + c * size, size), size)
        exponent = put_query_words(sums_ref[rows] + cross_ref[rows], out_ref, c)
        out_ref[c, width // LANES * size :] = exponent_rows(exponent)


def pack_kernel(place_ref, sums_ref, cross_ref, words_ref, parts_ref, out_ref):
    peers = out_ref.shape[0]
    half, width = sums_ref.shape
    size = half // (2 * peers)
    base = width // LANES * size
    totals = parts_ref[0]
    for c in range(1, parts_ref.shape[0]):
        totals = totals + parts_ref[c]
    totals = totals.reshape(-1, LANES)
    totals_exponent = exponents(totals)
    totals = as_words(totals, totals_exponent)
    for c in range(peers):
        rows = pl.ds(pl.multiple_of(place_ref[4] * (half // 2) + c * size, size), size)
        received = take_query_words(words_ref, c, scale_column(words_ref[c, base:], size), width)
        exponent = put_query_words(sums_ref[rows] + cross_ref[rows] + received, out_ref, c)
        out_ref[c, base : base + totals.shape[0]] = totals
        out_ref[c, base + totals.shape[0] :] = exponent_rows(jnp.concatenate([exponent, totals_exponent], axis=0))


def unpack_kernel(words_ref, query_ref, sums_ref):
    peers = words_ref.shape[0]
    size, width = query_ref.shape
    base = width // LANES * size
    count = sums_ref.shape[0]
    query, sums = 0.0, 0.0
    for c in range(peers):
        scale = scale_column(words_ref[c, base + count :], size + count)
        query = query + take_query_words(words_ref, c, scale[:size], width)
        sums = sums + words_ref[c, base : base + count].astype(i32).astype(f32) * scale[size:]
    query_ref[...] = query.astype(bf16)
    sums_ref[...] = sums


def join_kernel(place_ref, own_ref, beside_ref, cross_ref, corner_ref, out_ref, all_ref):
    core, side = place_ref[0], place_ref[4]
    all_ref[2 * core + side] = own_ref[...]
    all_ref[2 * core + 1 - side] = beside_ref[...]
    all_ref[2 - 2 * core + side] = cross_ref[...]
    all_ref[2 - 2 * core + 1 - side] = corner_ref[...]
    for j in range(3):
        rows = [all_ref[t // 2, 16 * j + t % 2 * 8 : 16 * j + t % 2 * 8 + 8] for t in range(8)]
        for m in range(4):
            out_ref[4 * j + m] = jnp.concatenate([row[:, 32 * m : 32 * m + 32] for row in rows], axis=1)


IN_VMEM = pl.BlockSpec(memory_space=pltpu.VMEM)
IN_SMEM = pl.BlockSpec(memory_space=pltpu.SMEM)


def call(kernel, shapes, args, flops, scratch=(), special=None, out_special=None, vmem=12):
    specs = [IN_VMEM] * len(args)
    for place, spec in (special or {}).items():
        specs[place] = spec
    many = isinstance(shapes, list)
    outs = [IN_VMEM] * (len(shapes) if many else 1)
    for place, spec in (out_special or {}).items():
        outs[place] = spec
    return pl.pallas_call(
        kernel,
        out_shape=shapes,
        in_specs=specs,
        out_specs=outs if many else outs[0],
        scratch_shapes=scratch,
        compiler_params=pltpu.CompilerParams(vmem_limit_bytes=vmem * 2**20),
        cost_estimate=pl.CostEstimate(flops=flops, bytes_accessed=2**16, transcendentals=0),
    )(*args)


def per_device(queries, codes, positives, codebook):
    swap = functools.partial(lax.ppermute, axis_name="core", perm=[(0, 1), (1, 0)])
    swap_x = functools.partial(lax.ppermute, axis_name="xl", perm=[(0, 1), (1, 0)])
    shape = jax.ShapeDtypeStruct
    own_codes = codes[0]
    subspaces, passage_count = own_codes.shape
    size, width = queries.shape[1:]
    chips = 16
    half = chips * size
    offset = lax.axis_index(("xl", "z", "core")) * passage_count
    axes = [lax.axis_index(name) for name in ("core", "xh", "y", "xl")]
    place = jnp.stack([axes[0], offset, *axes[1:]]).astype(i32)
    scalar = {0: IN_SMEM}
    length = width // LANES * size + 16
    own, share = call(
        spread_kernel,
        [shape((chips, length, LANES), bf16), shape((codebook.shape[0] // 2, *codebook.shape[1:]), bf16)],
        (place, queries[0], positives, codebook),
        10**6,
        special=scalar,
        vmem=60,
    )
    near = [share] + [lax.ppermute(share, "y", [(i, (i + k) % 4) for i in range(4)]) for k in range(1, 4)]
    near = jnp.stack(near)
    far = lax.ppermute(near, "xh", [(0, 1), (1, 0)])
    own = lax.all_to_all(own, CHIP, 0, 0)
    own, *books = lax.optimization_barrier((own, near, swap(near), far, swap(far)))
    other = swap(own)
    passages = call(
        decode_kernel,
        shape((width, passage_count), bf16),
        (place, own_codes, *books),
        10**6,
        special=scalar,
    )
    stats = call(scores_kernel, shape((32, 8, LANES), f32), (own, other, passages), 10**6)
    stats = lax.all_to_all(stats, CHIP + ("core",), 0, 0, tiled=True)
    query_other, query_own, grads = call(
        weights_kernel,
        [shape((half, width), f32), shape((half, width), f32), shape((width, passage_count), bf16)],
        (place, stats, own, other, passages),
        10**6,
        scratch=[pltpu.VMEM((2 * half, passage_count), bf16), pltpu.VMEM((2 * half, passage_count), bf16)],
        special=scalar,
        vmem=20,
    )
    query_cross = swap(query_other)

    def codeword_sums(mine):
        return call(
            functools.partial(codeword_kernel, mine),
            shape((8, 2, subspaces // 32, 16, LANES), f32),
            (place, grads, own_codes),
            10**6,
            special=scalar,
        )

    sums_cross = swap(codeword_sums(False))
    parts = codeword_sums(True) + sums_cross
    words = call(
        send_kernel, shape((chips // 2, length, LANES), i16), (place, query_own, query_cross), 10**6, special=scalar
    )
    parts, words = lax.optimization_barrier((parts, words))
    words = swap_x(words)
    parts = lax.all_to_all(parts.reshape(16, subspaces // 32, 16, LANES), SUB + ("xl",), 0, 0)
    count = subspaces // 32 * 16
    words = call(
        pack_kernel,
        shape((chips // 2, length + count, LANES), i16),
        (place, query_own, query_cross, words, parts),
        10**6,
        special=scalar,
    )
    words = lax.all_to_all(words, "z", 0, 0)
    query_grad, sums = call(unpack_kernel, [shape((size, width), bf16), shape((count, LANES), f32)], (words,), 10**6)
    beside = swap_x(sums)
    corner = lax.ppermute(sums, ("xl", "core"), [(i, 3 - i) for i in range(4)])
    cross = swap(sums)
    codeword_grad = call(
        join_kernel,
        shape((subspaces // 8, 8, 2 * LANES), f32),
        (place, sums, beside, cross, corner),
        10**6,
        scratch=[pltpu.VMEM((4, count, LANES), f32)],
        special=scalar,
    )
    return query_grad[None], codeword_grad


def solution(mesh):
    split = Mesh(mesh.devices.reshape(2, 8, 2, 2, 4), ("xl", "z", "core", "xh", "y"))
    blk = ("xl", "z", "core")
    return jax.shard_map(
        per_device,
        mesh=split,
        in_specs=(P(SUB, blk, None), P(SUB, None, blk), P(SUB, blk), P(SUB, None, None)),
        out_specs=(P(SUB, blk, None), P(SUB, None, None)),
        check_vma=False,
    )
```

```python
import functools

import jax
import jax.numpy as jnp
from jax import lax
from jax.experimental import pallas as pl
from jax.experimental.pallas import tpu as pltpu
from jax.sharding import Mesh, PartitionSpec as P

f32 = jnp.float32
bf16 = jnp.bfloat16
i32 = jnp.int32
i16 = jnp.int16
LANES = 128
BLOCK = 256
CHIP = ("xl", "z")
SUB = ("xh", "y")
ROWS_BY_ROWS = (((1,), (1,)), ((), ()))


def as_column(row):
    return jnp.transpose(jnp.broadcast_to(row, (LANES, row.shape[1])))[:, :1]


def as_row(column):
    return jnp.transpose(jnp.broadcast_to(column, (column.shape[0], LANES)))[:1]


def exponents(rows):
    peak = jnp.maximum(jnp.max(jnp.abs(rows), axis=1, keepdims=True), 2.0**-100)
    return jnp.ceil(jnp.log2(peak * (1.0 / 32767.0)))


def as_words(rows, exponent):
    scaled = jnp.round(rows * jnp.exp2(-exponent))
    return jnp.clip(scaled, -32767.0, 32767.0).astype(i32).astype(i16)


def exponent_rows(exponent):
    column = jnp.concatenate([exponent, jnp.zeros((LANES - exponent.shape[0], 1), f32)], axis=0)
    return jnp.transpose(jnp.broadcast_to(column, (LANES, LANES)))[:16].astype(i32).astype(i16)


def scale_column(rows, count):
    row = rows.astype(i32).astype(f32)[:1]
    return jnp.exp2(jnp.transpose(jnp.broadcast_to(row, (LANES, LANES)))[:count])


def spread_kernel(queries_ref, positives_ref, out_ref):
    size, width = queries_ref.shape
    target = jnp.concatenate([positives_ref[...], jnp.zeros((1, LANES - size), i32)], axis=1)
    tail = jnp.concatenate([target // LANES, target % LANES, jnp.zeros((14, LANES), i32)], axis=0)
    tail = tail.astype(f32).astype(bf16)
    for c in range(out_ref.shape[0]):
        for t in range(width // LANES):
            out_ref[c, t * size : (t + 1) * size] = queries_ref[:, t * LANES : (t + 1) * LANES]
        out_ref[c, width // LANES * size :] = tail


def share_kernel(place_ref, book_ref, share_ref):
    count = share_ref.shape[0]
    share_ref[...] = book_ref[pl.ds(place_ref[0] * count, count)]


def query_columns(pack_ref, t, first, count):
    size = (pack_ref.shape[1] - 16) // 6
    return pack_ref[first : first + count, t * size : (t + 1) * size, :].reshape(count * size, LANES)


def query_rows(pack_ref, first, count):
    return jnp.concatenate([query_columns(pack_ref, t, first, count) for t in range(6)], axis=1)


def target_columns(pack_ref):
    chips, length, _ = pack_ref.shape
    tail = pack_ref[:, length - 16 :, :].astype(f32)
    target = tail[:, 0, :] * LANES + tail[:, 1, :]
    target = jnp.concatenate([target, jnp.zeros((LANES - chips, LANES), f32)], axis=0)
    return jnp.transpose(target)


def decode_kernel(place_ref, codes_ref, near_ref, near_cross_ref, far_ref, far_cross_ref, out_ref):
    core, far_side, along = place_ref[0], 1 - place_ref[2], place_ref[3]
    share = near_ref.shape[1]

    def pair(j, carry):
        side, group, c, k = j // (4 * share), j // share % 4, j // (share // 2) % 2, j % (share // 2) * 2
        piece = (along + 4 - group) % 4
        rows = []
        for h in range(2):
            near = jnp.where(core == c, near_ref[piece, k + h].astype(f32), near_cross_ref[piece, k + h].astype(f32))
            far = jnp.where(core == c, far_ref[piece, k + h].astype(f32), far_cross_ref[piece, k + h].astype(f32))
            table = jnp.where(side == far_side, far, near)
            low, high = table[:, :LANES], table[:, LANES:]
            row = codes_ref[pl.ds(2 * j + h, 1), :]
            parts = []
            for t in range(row.shape[1] // LANES):
                code = jnp.broadcast_to(row[:, t * LANES : (t + 1) * LANES], (8, LANES))
                index = code & (LANES - 1)
                parts.append(
                    jnp.where(
                        code < LANES,
                        jnp.take_along_axis(low, index, axis=1, mode="promise_in_bounds"),
                        jnp.take_along_axis(high, index, axis=1, mode="promise_in_bounds"),
                    )
                )
            rows.append(jnp.concatenate(parts, axis=1))
        out_ref[pl.ds(pl.multiple_of(16 * j, 16), 16), :] = jnp.concatenate(rows, axis=0).astype(bf16)
        return carry

    lax.fori_loop(0, codes_ref.shape[0] // 2, pair, 0, unroll=8)


def local_logs(pack_ref, passages_ref):
    rows = []
    for b in range(2):
        tile = jnp.dot(query_rows(pack_ref, b * 8, 8), passages_ref[...], preferred_element_type=f32)
        peak = jnp.max(tile, axis=1, keepdims=True)
        total = jnp.sum(jnp.exp(tile - peak), axis=1, keepdims=True)
        row = as_row(peak + jnp.log(total))
        rows += [row[:, j * LANES : (j + 1) * LANES] for j in range(2)]
    return jnp.concatenate(rows, axis=0)


def own_scores_kernel(pack_ref, passages_ref, logs_ref):
    logs_ref[...] = local_logs(pack_ref, passages_ref)


def other_scores_kernel(pack_ref, passages_ref, own_logs_ref, stats_ref):
    logs = jnp.concatenate([own_logs_ref[...], local_logs(pack_ref, passages_ref)], axis=0)
    stats_ref[...] = jnp.broadcast_to(logs[None], stats_ref.shape)


def log_totals(core, stats_ref, h):
    peers = stats_ref.shape[0]
    same = (lax.broadcasted_iota(i32, (peers, LANES), 0) & 1) == core
    out = []
    for j in range(4):
        logs = jnp.where(same, stats_ref[:, 4 * h + j, :], stats_ref[:, 4 - 4 * h + j, :])
        peak = jnp.max(logs, axis=0, keepdims=True)
        out.append(peak + jnp.log(jnp.sum(jnp.exp(logs - peak), axis=0, keepdims=True)))
    return out


def weights_kernel(
    place_ref, stats_ref, own_ref, other_ref, passages_ref, other_sums_ref, own_sums_ref, grads_ref,
    high_ref, low_ref, turned_ref
):
    core, offset = place_ref[0], place_ref[1]
    half, passage_count = own_sums_ref.shape[0], passages_ref.shape[1]
    size = half // own_ref.shape[0]
    passages = passages_ref[...]
    spot = lax.broadcasted_iota(i32, (size, passage_count), 1) + offset
    for h, pack_ref, sums_ref in ((1, other_ref, other_sums_ref), (0, own_ref, own_sums_ref)):
        for t in range(turned_ref.shape[0] // LANES):
            columns = query_columns(pack_ref, t, 0, pack_ref.shape[0])
            turned_ref[t * LANES : (t + 1) * LANES, h * half : (h + 1) * half] = jnp.transpose(columns)
        totals = [as_column(row) for row in log_totals(core, stats_ref, h)]
        targets = target_columns(pack_ref)[:size].astype(i32)
        for b in range(half // BLOCK):
            tile = jnp.dot(query_rows(pack_ref, b * 8, 8), passages, preferred_element_type=f32)
            tile = jnp.exp(tile - jnp.concatenate(totals[2 * b : 2 * b + 2], axis=0))
            rows = slice(h * half + b * BLOCK, h * half + (b + 1) * BLOCK)
            pieces = []
            for c in range(BLOCK // size):
                place = b * BLOCK // size + c
                hits = jnp.where(targets[:, place : place + 1] == spot, 1.0, 0.0)
                pieces.append(tile[c * size : (c + 1) * size] - hits)
            weight = jnp.concatenate(pieces, axis=0)
            high = weight.astype(bf16)
            low = (weight - high.astype(f32)).astype(bf16)
            high_ref[rows] = high
            low_ref[rows] = low
            sums_ref[b * BLOCK : (b + 1) * BLOCK] = lax.dot_general(
                high, passages, ROWS_BY_ROWS, preferred_element_type=f32
            ) + lax.dot_general(low, passages, ROWS_BY_ROWS, preferred_element_type=f32)
    for n in range(passage_count // BLOCK):
        columns = slice(n * BLOCK, (n + 1) * BLOCK)
        grad = jnp.dot(turned_ref[...], high_ref[:, columns], preferred_element_type=f32) + jnp.dot(
            turned_ref[...], low_ref[:, columns], preferred_element_type=f32
        )
        grads_ref[:, columns] = grad.astype(bf16)


def codeword_kernel(mine, place_ref, grads_ref, codes_ref, out_ref):
    core = place_ref[0] if mine else 1 - place_ref[0]
    word = lax.broadcasted_iota(i32, (64, codes_ref.shape[1]), 0)

    def two(j, carry):
        first = j // 3 * 12 + 6 * core + 2 * (j % 3)
        grads = grads_ref[pl.ds(pl.multiple_of(8 * first, 16), 16), :].astype(f32)
        sums = []
        for m in range(2):
            grad = grads[8 * m : 8 * m + 8]
            code = codes_ref[pl.ds(first + m, 1), :]
            high = code >> 6
            parts = jnp.concatenate([jnp.where(high == t, grad, 0.0) for t in range(4)], axis=0).astype(bf16)
            onehot = jnp.where((code & 63) == word, 1.0, 0.0).astype(bf16)
            sums.append(lax.dot_general(parts, onehot, ROWS_BY_ROWS, preferred_element_type=f32))
        sums = jnp.concatenate(sums, axis=1)
        for k in range(2):
            out_ref[j // 3, k, j % 3] = sums[16 * k : 16 * k + 16]
        return carry

    lax.fori_loop(0, codes_ref.shape[0] // 4, two, 0, unroll=8)


def put_query_words(chunk, out_ref, c):
    size, width = chunk.shape
    exponent = exponents(chunk)
    words = as_words(chunk, exponent)
    for t in range(width // LANES):
        out_ref[c, t * size : (t + 1) * size] = words[:, t * LANES : (t + 1) * LANES]
    return exponent


def take_query_words(words_ref, c, scale, width):
    size = scale.shape[0]
    words = [words_ref[c, t * size : (t + 1) * size] for t in range(width // LANES)]
    return jnp.concatenate([word.astype(i32).astype(f32) * scale for word in words], axis=1)


def send_kernel(place_ref, sums_ref, cross_ref, out_ref):
    peers = out_ref.shape[0]
    half, width = sums_ref.shape
    size = half // (2 * peers)
    for c in range(peers):
        rows = pl.ds(pl.multiple_of((1 - place_ref[4]) * (half // 2) + c * size, size), size)
        exponent = put_query_words(sums_ref[rows] + cross_ref[rows], out_ref, c)
        out_ref[c, width // LANES * size :] = exponent_rows(exponent)


def pack_kernel(place_ref, sums_ref, cross_ref, words_ref, parts_ref, out_ref):
    peers = out_ref.shape[0]
    half, width = sums_ref.shape
    size = half // (2 * peers)
    base = width // LANES * size
    totals = parts_ref[0]
    for c in range(1, parts_ref.shape[0]):
        totals = totals + parts_ref[c]
    totals = totals.reshape(-1, LANES)
    totals_exponent = exponents(totals)
    totals = as_words(totals, totals_exponent)
    for c in range(peers):
        rows = pl.ds(pl.multiple_of(place_ref[4] * (half // 2) + c * size, size), size)
        received = take_query_words(words_ref, c, scale_column(words_ref[c, base:], size), width)
        exponent = put_query_words(sums_ref[rows] + cross_ref[rows] + received, out_ref, c)
        out_ref[c, base : base + totals.shape[0]] = totals
        out_ref[c, base + totals.shape[0] :] = exponent_rows(jnp.concatenate([exponent, totals_exponent], axis=0))


def unpack_kernel(words_ref, query_ref, sums_ref):
    peers = words_ref.shape[0]
    size, width = query_ref.shape
    base = width // LANES * size
    count = sums_ref.shape[0]
    query, sums = 0.0, 0.0
    for c in range(peers):
        scale = scale_column(words_ref[c, base + count :], size + count)
        query = query + take_query_words(words_ref, c, scale[:size], width)
        sums = sums + words_ref[c, base : base + count].astype(i32).astype(f32) * scale[size:]
    query_ref[...] = query.astype(bf16)
    sums_ref[...] = sums


def join_kernel(place_ref, own_ref, beside_ref, cross_ref, corner_ref, out_ref, all_ref):
    core, side = place_ref[0], place_ref[4]
    all_ref[2 * core + side] = own_ref[...]
    all_ref[2 * core + 1 - side] = beside_ref[...]
    all_ref[2 - 2 * core + side] = cross_ref[...]
    all_ref[2 - 2 * core + 1 - side] = corner_ref[...]
    for c in range(2):
        for j in range(3):
            rows = [all_ref[2 * c + t // 2, 16 * j + t % 2 * 8 : 16 * j + t % 2 * 8 + 8] for t in range(4)]
            for m in range(2):
                out_ref[6 * c + 2 * j + m] = jnp.concatenate([row[:, 64 * m : 64 * m + 64] for row in rows], axis=1)


IN_VMEM = pl.BlockSpec(memory_space=pltpu.VMEM)
IN_SMEM = pl.BlockSpec(memory_space=pltpu.SMEM)


def call(kernel, shapes, args, flops, scratch=(), special=None, out_special=None, vmem=12):
    specs = [IN_VMEM] * len(args)
    for place, spec in (special or {}).items():
        specs[place] = spec
    many = isinstance(shapes, list)
    outs = [IN_VMEM] * (len(shapes) if many else 1)
    for place, spec in (out_special or {}).items():
        outs[place] = spec
    return pl.pallas_call(
        kernel,
        out_shape=shapes,
        in_specs=specs,
        out_specs=outs if many else outs[0],
        scratch_shapes=scratch,
        compiler_params=pltpu.CompilerParams(vmem_limit_bytes=vmem * 2**20),
        cost_estimate=pl.CostEstimate(flops=flops, bytes_accessed=2**16, transcendentals=0),
    )(*args)


def per_device(queries, codes, positives, codebook):
    swap = functools.partial(lax.ppermute, axis_name="core", perm=[(0, 1), (1, 0)])
    swap_x = functools.partial(lax.ppermute, axis_name="xl", perm=[(0, 1), (1, 0)])
    shape = jax.ShapeDtypeStruct
    own_codes = codes[0]
    subspaces, passage_count = own_codes.shape
    size, width = queries.shape[1:]
    chips = 16
    half = chips * size
    offset = lax.axis_index(("xl", "z", "core")) * passage_count
    axes = [lax.axis_index(name) for name in ("core", "xh", "y", "xl")]
    place = jnp.stack([axes[0], offset, *axes[1:]]).astype(i32)
    scalar = {0: IN_SMEM}
    length = width // LANES * size + 16
    own = call(spread_kernel, shape((chips, length, LANES), bf16), (queries[0], positives), 10**6, vmem=60)
    share = call(
        share_kernel,
        shape((codebook.shape[0] // 2, *codebook.shape[1:]), bf16),
        (place, codebook),
        10**6,
        special=scalar,
    )
    near = [share] + [lax.ppermute(share, "y", [(i, (i + k) % 4) for i in range(4)]) for k in range(1, 4)]
    near = jnp.stack(near)
    far = lax.ppermute(near, "xh", [(0, 1), (1, 0)])
    own = lax.all_to_all(own, CHIP, 0, 0)
    passages = call(
        decode_kernel,
        shape((width, passage_count), bf16),
        (place, own_codes, near, swap(near), far, swap(far)),
        10**6,
        special=scalar,
    )
    own, passages = lax.optimization_barrier((own, passages))
    other = swap(own)
    own_logs = call(own_scores_kernel, shape((4, LANES), f32), (own, passages), 10**6)
    stats = call(other_scores_kernel, shape((32, 8, LANES), f32), (other, passages, own_logs), 10**6)
    stats = lax.all_to_all(stats, CHIP + ("core",), 0, 0, tiled=True)
    query_other, query_own, grads = call(
        weights_kernel,
        [shape((half, width), f32), shape((half, width), f32), shape((width, passage_count), bf16)],
        (place, stats, own, other, passages),
        10**6,
        scratch=[
            pltpu.VMEM((2 * half, passage_count), bf16),
            pltpu.VMEM((2 * half, passage_count), bf16),
            pltpu.VMEM((width, 2 * half), bf16),
        ],
        special=scalar,
        vmem=20,
    )
    query_cross = swap(query_other)

    def codeword_sums(mine):
        return call(
            functools.partial(codeword_kernel, mine),
            shape((8, 2, subspaces // 32, 16, LANES), f32),
            (place, grads, own_codes),
            10**6,
            special=scalar,
        )

    sums_cross = swap(codeword_sums(False))
    parts = codeword_sums(True) + sums_cross
    words = call(
        send_kernel, shape((chips // 2, length, LANES), i16), (place, query_own, query_cross), 10**6, special=scalar
    )
    parts, words = lax.optimization_barrier((parts, words))
    words = swap_x(words)
    parts = lax.all_to_all(parts.reshape(16, subspaces // 32, 16, LANES), SUB + ("xl",), 0, 0)
    count = subspaces // 32 * 16
    words = call(
        pack_kernel,
        shape((chips // 2, length + count, LANES), i16),
        (place, query_own, query_cross, words, parts),
        10**6,
        special=scalar,
    )
    words = lax.all_to_all(words, "z", 0, 0)
    query_grad, sums = call(unpack_kernel, [shape((size, width), bf16), shape((count, LANES), f32)], (words,), 10**6)
    beside = swap_x(sums)
    corner = lax.ppermute(sums, ("xl", "core"), [(i, 3 - i) for i in range(4)])
    cross = swap(sums)
    codeword_grad = call(
        join_kernel,
        shape((subspaces // 8, 8, 2 * LANES), f32),
        (place, sums, beside, cross, corner),
        10**6,
        scratch=[pltpu.VMEM((4, count, LANES), f32)],
        special=scalar,
    )
    return query_grad[None], codeword_grad


def solution(mesh):
    split = Mesh(mesh.devices.reshape(2, 8, 2, 2, 4), ("xl", "z", "core", "xh", "y"))
    blk = ("xl", "z", "core")
    return jax.shard_map(
        per_device,
        mesh=split,
        in_specs=(P(SUB, blk, None), P(SUB, None, blk), P(SUB, blk), P(SUB, None, None)),
        out_specs=(P(SUB, blk, None), P(SUB, None, None)),
        check_vma=False,
    )
```

```python
import functools

import jax
import jax.numpy as jnp
from jax import lax
from jax.experimental import pallas as pl
from jax.experimental.pallas import tpu as pltpu
from jax.sharding import Mesh, PartitionSpec as P

f32 = jnp.float32
bf16 = jnp.bfloat16
i32 = jnp.int32
i16 = jnp.int16
LANES = 128
BLOCK = 256
CHIP = ("xl", "z")
SUB = ("xh", "y")
ROWS_BY_ROWS = (((1,), (1,)), ((), ()))


def as_column(row):
    return jnp.transpose(jnp.broadcast_to(row, (LANES, row.shape[1])))[:, :1]


def as_row(column):
    return jnp.transpose(jnp.broadcast_to(column, (column.shape[0], LANES)))[:1]


def exponents(rows):
    peak = jnp.maximum(jnp.max(jnp.abs(rows), axis=1, keepdims=True), 2.0**-100)
    return jnp.ceil(jnp.log2(peak * (1.0 / 32767.0)))


def as_words(rows, exponent):
    scaled = jnp.round(rows * jnp.exp2(-exponent))
    return jnp.clip(scaled, -32767.0, 32767.0).astype(i32).astype(i16)


def exponent_rows(exponent):
    column = jnp.concatenate([exponent, jnp.zeros((LANES - exponent.shape[0], 1), f32)], axis=0)
    return jnp.transpose(jnp.broadcast_to(column, (LANES, LANES)))[:16].astype(i32).astype(i16)


def scale_column(rows, count):
    row = rows.astype(i32).astype(f32)[:1]
    return jnp.exp2(jnp.transpose(jnp.broadcast_to(row, (LANES, LANES)))[:count])


def spread_kernel(queries_ref, positives_ref, out_ref, block_ref, sems):
    size, width = queries_ref.shape
    target = jnp.concatenate([positives_ref[...], jnp.zeros((1, LANES - size), i32)], axis=1)
    tail = jnp.concatenate([target // LANES, target % LANES, jnp.zeros((14, LANES), i32)], axis=0)
    for t in range(width // LANES):
        block_ref[t * size : (t + 1) * size] = queries_ref[:, t * LANES : (t + 1) * LANES]
    block_ref[width // LANES * size :] = tail.astype(f32).astype(bf16)
    sends = [pltpu.make_async_copy(block_ref, out_ref.at[c], sems.at[c]) for c in range(out_ref.shape[0])]
    for send in sends:
        send.start()
    for send in sends:
        send.wait()


def share_kernel(place_ref, book_ref, share_ref):
    count = share_ref.shape[0]
    share_ref[...] = book_ref[pl.ds(place_ref[0] * count, count)]


def query_columns(pack_ref, t, first, count):
    size = (pack_ref.shape[1] - 16) // 6
    return pack_ref[first : first + count, t * size : (t + 1) * size, :].reshape(count * size, LANES)


def query_rows(pack_ref, first, count):
    return jnp.concatenate([query_columns(pack_ref, t, first, count) for t in range(6)], axis=1)


def target_columns(pack_ref):
    chips, length, _ = pack_ref.shape
    tail = pack_ref[:, length - 16 :, :].astype(f32)
    target = tail[:, 0, :] * LANES + tail[:, 1, :]
    target = jnp.concatenate([target, jnp.zeros((LANES - chips, LANES), f32)], axis=0)
    return jnp.transpose(target)


def decode_kernel(place_ref, codes_ref, near_ref, near_cross_ref, far_ref, far_cross_ref, out_ref):
    core, far_side, along = place_ref[0], 1 - place_ref[2], place_ref[3]
    share = near_ref.shape[1]

    def pair(j, carry):
        side, group, c, k = j // (4 * share), j // share % 4, j // (share // 2) % 2, j % (share // 2) * 2
        piece = (along + 4 - group) % 4
        rows = []
        for h in range(2):
            near = jnp.where(core == c, near_ref[piece, k + h].astype(f32), near_cross_ref[piece, k + h].astype(f32))
            far = jnp.where(core == c, far_ref[piece, k + h].astype(f32), far_cross_ref[piece, k + h].astype(f32))
            table = jnp.where(side == far_side, far, near)
            low, high = table[:, :LANES], table[:, LANES:]
            row = codes_ref[pl.ds(2 * j + h, 1), :]
            parts = []
            for t in range(row.shape[1] // LANES):
                code = jnp.broadcast_to(row[:, t * LANES : (t + 1) * LANES], (8, LANES))
                index = code & (LANES - 1)
                parts.append(
                    jnp.where(
                        code < LANES,
                        jnp.take_along_axis(low, index, axis=1, mode="promise_in_bounds"),
                        jnp.take_along_axis(high, index, axis=1, mode="promise_in_bounds"),
                    )
                )
            rows.append(jnp.concatenate(parts, axis=1))
        out_ref[pl.ds(pl.multiple_of(16 * j, 16), 16), :] = jnp.concatenate(rows, axis=0).astype(bf16)
        return carry

    lax.fori_loop(0, codes_ref.shape[0] // 2, pair, 0, unroll=8)


def local_logs(pack_ref, passages_ref):
    rows = []
    for b in range(2):
        tile = jnp.dot(query_rows(pack_ref, b * 8, 8), passages_ref[...], preferred_element_type=f32)
        peak = jnp.max(tile, axis=1, keepdims=True)
        total = jnp.sum(jnp.exp(tile - peak), axis=1, keepdims=True)
        row = as_row(peak + jnp.log(total))
        rows += [row[:, j * LANES : (j + 1) * LANES] for j in range(2)]
    return jnp.concatenate(rows, axis=0)


def own_scores_kernel(pack_ref, passages_ref, logs_ref):
    logs_ref[...] = local_logs(pack_ref, passages_ref)


def other_scores_kernel(pack_ref, passages_ref, own_logs_ref, stats_ref):
    logs = jnp.concatenate([own_logs_ref[...], local_logs(pack_ref, passages_ref)], axis=0)
    stats_ref[...] = jnp.broadcast_to(logs[None], stats_ref.shape)


def log_totals(core, stats_ref, h):
    peers = stats_ref.shape[0]
    same = (lax.broadcasted_iota(i32, (peers, LANES), 0) & 1) == core
    out = []
    for j in range(4):
        logs = jnp.where(same, stats_ref[:, 4 * h + j, :], stats_ref[:, 4 - 4 * h + j, :])
        peak = jnp.max(logs, axis=0, keepdims=True)
        out.append(peak + jnp.log(jnp.sum(jnp.exp(logs - peak), axis=0, keepdims=True)))
    return out


def weights_kernel(
    place_ref, stats_ref, own_ref, other_ref, passages_ref, other_sums_ref, own_sums_ref, grads_ref,
    high_ref, low_ref, turned_ref
):
    core, offset = place_ref[0], place_ref[1]
    half, passage_count = own_sums_ref.shape[0], passages_ref.shape[1]
    size = half // own_ref.shape[0]
    passages = passages_ref[...]
    spot = lax.broadcasted_iota(i32, (size, passage_count), 1) + offset
    for h, pack_ref, sums_ref in ((1, other_ref, other_sums_ref), (0, own_ref, own_sums_ref)):
        for t in range(turned_ref.shape[0] // LANES):
            columns = query_columns(pack_ref, t, 0, pack_ref.shape[0])
            turned_ref[t * LANES : (t + 1) * LANES, h * half : (h + 1) * half] = jnp.transpose(columns)
        totals = [as_column(row) for row in log_totals(core, stats_ref, h)]
        targets = target_columns(pack_ref)[:size].astype(i32)
        for b in range(half // BLOCK):
            tile = jnp.dot(query_rows(pack_ref, b * 8, 8), passages, preferred_element_type=f32)
            tile = jnp.exp(tile - jnp.concatenate(totals[2 * b : 2 * b + 2], axis=0))
            rows = slice(h * half + b * BLOCK, h * half + (b + 1) * BLOCK)
            pieces = []
            for c in range(BLOCK // size):
                place = b * BLOCK // size + c
                hits = jnp.where(targets[:, place : place + 1] == spot, 1.0, 0.0)
                pieces.append(tile[c * size : (c + 1) * size] - hits)
            weight = jnp.concatenate(pieces, axis=0)
            high = weight.astype(bf16)
            low = (weight - high.astype(f32)).astype(bf16)
            high_ref[rows] = high
            low_ref[rows] = low
            sums_ref[b * BLOCK : (b + 1) * BLOCK] = lax.dot_general(
                high, passages, ROWS_BY_ROWS, preferred_element_type=f32
            ) + lax.dot_general(low, passages, ROWS_BY_ROWS, preferred_element_type=f32)
    for n in range(passage_count // BLOCK):
        columns = slice(n * BLOCK, (n + 1) * BLOCK)
        grad = jnp.dot(turned_ref[...], high_ref[:, columns], preferred_element_type=f32) + jnp.dot(
            turned_ref[...], low_ref[:, columns], preferred_element_type=f32
        )
        grads_ref[:, columns] = grad.astype(bf16)


def codeword_sums(core, grads_ref, codes_ref, out_ref):
    word = lax.broadcasted_iota(i32, (64, codes_ref.shape[1]), 0)

    def two(j, carry):
        first = j // 3 * 12 + 6 * core + 2 * (j % 3)
        grads = grads_ref[pl.ds(pl.multiple_of(8 * first, 16), 16), :].astype(f32)
        sums = []
        for m in range(2):
            grad = grads[8 * m : 8 * m + 8]
            code = codes_ref[pl.ds(first + m, 1), :]
            high = code >> 6
            parts = jnp.concatenate([jnp.where(high == t, grad, 0.0) for t in range(4)], axis=0).astype(bf16)
            onehot = jnp.where((code & 63) == word, 1.0, 0.0).astype(bf16)
            sums.append(lax.dot_general(parts, onehot, ROWS_BY_ROWS, preferred_element_type=f32))
        sums = jnp.concatenate(sums, axis=1)
        for k in range(2):
            out_ref[j // 3, k, j % 3] = sums[16 * k : 16 * k + 16]
        return carry

    lax.fori_loop(0, codes_ref.shape[0] // 4, two, 0, unroll=8)


def codeword_kernel(place_ref, grads_ref, codes_ref, out_ref):
    codeword_sums(1 - place_ref[0], grads_ref, codes_ref, out_ref)


def put_query_words(chunk, out_ref, c):
    size, width = chunk.shape
    exponent = exponents(chunk)
    words = as_words(chunk, exponent)
    for t in range(width // LANES):
        out_ref[c, t * size : (t + 1) * size] = words[:, t * LANES : (t + 1) * LANES]
    return exponent


def take_query_words(words_ref, c, scale, width):
    size = scale.shape[0]
    words = [words_ref[c, t * size : (t + 1) * size] for t in range(width // LANES)]
    return jnp.concatenate([word.astype(i32).astype(f32) * scale for word in words], axis=1)


def send_kernel(place_ref, grads_ref, codes_ref, sums_ref, cross_ref, parts_ref, out_ref):
    peers = out_ref.shape[0]
    half, width = sums_ref.shape
    size = half // (2 * peers)
    for c in range(peers):
        rows = pl.ds(pl.multiple_of((1 - place_ref[4]) * (half // 2) + c * size, size), size)
        exponent = put_query_words(sums_ref[rows] + cross_ref[rows], out_ref, c)
        out_ref[c, width // LANES * size :] = exponent_rows(exponent)
    codeword_sums(place_ref[0], grads_ref, codes_ref, parts_ref)


def pack_kernel(place_ref, sums_ref, cross_ref, words_ref, parts_ref, out_ref):
    peers = out_ref.shape[0]
    half, width = sums_ref.shape
    size = half // (2 * peers)
    base = width // LANES * size
    totals = parts_ref[0]
    for c in range(1, parts_ref.shape[0]):
        totals = totals + parts_ref[c]
    totals = totals.reshape(-1, LANES)
    totals_exponent = exponents(totals)
    totals = as_words(totals, totals_exponent)
    for c in range(peers):
        rows = pl.ds(pl.multiple_of(place_ref[4] * (half // 2) + c * size, size), size)
        received = take_query_words(words_ref, c, scale_column(words_ref[c, base:], size), width)
        exponent = put_query_words(sums_ref[rows] + cross_ref[rows] + received, out_ref, c)
        out_ref[c, base : base + totals.shape[0]] = totals
        out_ref[c, base + totals.shape[0] :] = exponent_rows(jnp.concatenate([exponent, totals_exponent], axis=0))


def unpack_query_kernel(words_ref, query_ref):
    peers, length, _ = words_ref.shape
    size, width = query_ref.shape
    query = 0.0
    for c in range(peers):
        query = query + take_query_words(words_ref, c, scale_column(words_ref[c, length - 16 :], size), width)
    query_ref[...] = query.astype(bf16)


def unpack_sums_kernel(size, words_ref, sums_ref):
    peers, length, _ = words_ref.shape
    count = sums_ref.shape[0]
    start = length - 16 - count
    sums = 0.0
    for c in range(peers):
        scale = scale_column(words_ref[c, length - 16 :], size + count)[size:]
        sums = sums + words_ref[c, start : start + count].astype(i32).astype(f32) * scale
    sums_ref[...] = sums


def join_kernel(place_ref, own_ref, beside_ref, cross_ref, corner_ref, out_ref, all_ref):
    core, side = place_ref[0], place_ref[4]
    all_ref[2 * core + side] = own_ref[...]
    all_ref[2 * core + 1 - side] = beside_ref[...]
    all_ref[2 - 2 * core + side] = cross_ref[...]
    all_ref[2 - 2 * core + 1 - side] = corner_ref[...]
    for c in range(2):
        for j in range(3):
            rows = [all_ref[2 * c + t // 2, 16 * j + t % 2 * 8 : 16 * j + t % 2 * 8 + 8] for t in range(4)]
            for m in range(2):
                out_ref[6 * c + 2 * j + m] = jnp.concatenate([row[:, 64 * m : 64 * m + 64] for row in rows], axis=1)


IN_VMEM = pl.BlockSpec(memory_space=pltpu.VMEM)
ANYWHERE = pl.BlockSpec(memory_space=pl.ANY)
IN_SMEM = pl.BlockSpec(memory_space=pltpu.SMEM)


def call(kernel, shapes, args, flops, scratch=(), special=None, out_special=None, vmem=12):
    specs = [IN_VMEM] * len(args)
    for place, spec in (special or {}).items():
        specs[place] = spec
    many = isinstance(shapes, list)
    outs = [IN_VMEM] * (len(shapes) if many else 1)
    for place, spec in (out_special or {}).items():
        outs[place] = spec
    return pl.pallas_call(
        kernel,
        out_shape=shapes,
        in_specs=specs,
        out_specs=outs if many else outs[0],
        scratch_shapes=scratch,
        compiler_params=pltpu.CompilerParams(vmem_limit_bytes=vmem * 2**20),
        cost_estimate=pl.CostEstimate(flops=flops, bytes_accessed=2**16, transcendentals=0),
    )(*args)


def per_device(queries, codes, positives, codebook):
    swap = functools.partial(lax.ppermute, axis_name="core", perm=[(0, 1), (1, 0)])
    swap_x = functools.partial(lax.ppermute, axis_name="xl", perm=[(0, 1), (1, 0)])
    shape = jax.ShapeDtypeStruct
    own_codes = codes[0]
    subspaces, passage_count = own_codes.shape
    size, width = queries.shape[1:]
    chips = 16
    half = chips * size
    offset = lax.axis_index(("xl", "z", "core")) * passage_count
    axes = [lax.axis_index(name) for name in ("core", "xh", "y", "xl")]
    place = jnp.stack([axes[0], offset, *axes[1:]]).astype(i32)
    scalar = {0: IN_SMEM}
    length = width // LANES * size + 16
    own = call(
        spread_kernel,
        shape((chips, length, LANES), bf16),
        (queries[0], positives),
        10**6,
        scratch=[pltpu.VMEM((length, LANES), bf16), pltpu.SemaphoreType.DMA((chips,))],
        out_special={0: ANYWHERE},
        vmem=60,
    )
    share = call(
        share_kernel,
        shape((codebook.shape[0] // 2, *codebook.shape[1:]), bf16),
        (place, codebook),
        10**6,
        special=scalar,
    )
    near = [share] + [lax.ppermute(share, "y", [(i, (i + k) % 4) for i in range(4)]) for k in range(1, 4)]
    near = jnp.stack(near)
    far = lax.ppermute(near, "xh", [(0, 1), (1, 0)])
    own = lax.all_to_all(own, CHIP, 0, 0)
    passages = call(
        decode_kernel,
        shape((width, passage_count), bf16),
        (place, own_codes, near, swap(near), far, swap(far)),
        10**6,
        special=scalar,
    )
    own, passages = lax.optimization_barrier((own, passages))
    other = swap(own)
    own_logs = call(own_scores_kernel, shape((4, LANES), f32), (own, passages), 10**6)
    stats = call(other_scores_kernel, shape((32, 8, LANES), f32), (other, passages, own_logs), 10**6)
    stats = lax.all_to_all(stats, CHIP + ("core",), 0, 0, tiled=True)
    query_other, query_own, grads = call(
        weights_kernel,
        [shape((half, width), f32), shape((half, width), f32), shape((width, passage_count), bf16)],
        (place, stats, own, other, passages),
        10**6,
        scratch=[
            pltpu.VMEM((2 * half, passage_count), bf16),
            pltpu.VMEM((2 * half, passage_count), bf16),
            pltpu.VMEM((width, 2 * half), bf16),
        ],
        special=scalar,
        vmem=20,
    )
    query_cross = swap(query_other)

    sums_shape = shape((8, 2, subspaces // 32, 16, LANES), f32)
    parts_cross = swap(call(codeword_kernel, sums_shape, (place, grads, own_codes), 10**6, special=scalar))
    parts, words = call(
        send_kernel,
        [sums_shape, shape((chips // 2, length, LANES), i16)],
        (place, grads, own_codes, query_own, query_cross),
        10**6,
        special=scalar,
    )
    parts = parts + parts_cross
    parts, words = lax.optimization_barrier((parts, words))
    words = swap_x(words)
    parts = lax.all_to_all(parts.reshape(16, subspaces // 32, 16, LANES), SUB + ("xl",), 0, 0)
    count = subspaces // 32 * 16
    words = call(
        pack_kernel,
        shape((chips // 2, length + count, LANES), i16),
        (place, query_own, query_cross, words, parts),
        10**6,
        special=scalar,
    )
    words = lax.all_to_all(words, "z", 0, 0)
    sums = call(functools.partial(unpack_sums_kernel, size), shape((count, LANES), f32), (words,), 10**6)
    beside = swap_x(sums)
    corner = lax.ppermute(sums, ("xl", "core"), [(i, 3 - i) for i in range(4)])
    cross = swap(sums)
    query_grad = call(unpack_query_kernel, shape((size, width), bf16), (words,), 10**6)
    codeword_grad = call(
        join_kernel,
        shape((subspaces // 8, 8, 2 * LANES), f32),
        (place, sums, beside, cross, corner),
        10**6,
        scratch=[pltpu.VMEM((4, count, LANES), f32)],
        special=scalar,
    )
    return query_grad[None], codeword_grad


def solution(mesh):
    split = Mesh(mesh.devices.reshape(2, 8, 2, 2, 4), ("xl", "z", "core", "xh", "y"))
    blk = ("xl", "z", "core")
    return jax.shard_map(
        per_device,
        mesh=split,
        in_specs=(P(SUB, blk, None), P(SUB, None, blk), P(SUB, blk), P(SUB, None, None)),
        out_specs=(P(SUB, blk, None), P(SUB, None, None)),
        check_vma=False,
    )
```

```python
import functools

import jax
import jax.numpy as jnp
from jax import lax
from jax.experimental import pallas as pl
from jax.experimental.pallas import tpu as pltpu
from jax.sharding import Mesh, PartitionSpec as P

f32 = jnp.float32
bf16 = jnp.bfloat16
i32 = jnp.int32
i16 = jnp.int16
LANES = 128
BLOCK = 256
CHIP = ("xl", "z")
SUB = ("xh", "y")
ROWS_BY_ROWS = (((1,), (1,)), ((), ()))


def as_column(row):
    return jnp.transpose(jnp.broadcast_to(row, (LANES, row.shape[1])))[:, :1]


def as_row(column):
    return jnp.transpose(jnp.broadcast_to(column, (column.shape[0], LANES)))[:1]


def exponents(rows):
    peak = jnp.maximum(jnp.max(jnp.abs(rows), axis=1, keepdims=True), 2.0**-100)
    return jnp.ceil(jnp.log2(peak * (1.0 / 32767.0)))


def as_words(rows, exponent):
    scaled = jnp.round(rows * jnp.exp2(-exponent))
    return jnp.clip(scaled, -32767.0, 32767.0).astype(i32).astype(i16)


def exponent_rows(exponent):
    column = jnp.concatenate([exponent, jnp.zeros((LANES - exponent.shape[0], 1), f32)], axis=0)
    return jnp.transpose(jnp.broadcast_to(column, (LANES, LANES)))[:16].astype(i32).astype(i16)


def scale_column(rows, count):
    row = rows.astype(i32).astype(f32)[:1]
    return jnp.exp2(jnp.transpose(jnp.broadcast_to(row, (LANES, LANES)))[:count])


def spread_kernel(queries_ref, positives_ref, out_ref, block_ref, sems):
    size, width = queries_ref.shape
    target = jnp.concatenate([positives_ref[...], jnp.zeros((1, LANES - size), i32)], axis=1)
    tail = jnp.concatenate([target // LANES, target % LANES, jnp.zeros((14, LANES), i32)], axis=0)
    for t in range(width // LANES):
        block_ref[t * size : (t + 1) * size] = queries_ref[:, t * LANES : (t + 1) * LANES]
    block_ref[width // LANES * size :] = tail.astype(f32).astype(bf16)
    sends = [pltpu.make_async_copy(block_ref, out_ref.at[c], sems.at[c]) for c in range(out_ref.shape[0])]
    for send in sends:
        send.start()
    for send in sends:
        send.wait()


def share_kernel(place_ref, book_ref, share_ref):
    count = share_ref.shape[0]
    share_ref[...] = book_ref[pl.ds(place_ref[0] * count, count)]


def query_columns(pack_ref, t, first, count):
    size = (pack_ref.shape[1] - 16) // 6
    return pack_ref[first : first + count, t * size : (t + 1) * size, :].reshape(count * size, LANES)


def query_rows(pack_ref, first, count):
    return jnp.concatenate([query_columns(pack_ref, t, first, count) for t in range(6)], axis=1)


def target_columns(pack_ref):
    chips, length, _ = pack_ref.shape
    tail = pack_ref[:, length - 16 :, :].astype(f32)
    target = tail[:, 0, :] * LANES + tail[:, 1, :]
    target = jnp.concatenate([target, jnp.zeros((LANES - chips, LANES), f32)], axis=0)
    return jnp.transpose(target)


def decode_kernel(place_ref, codes_ref, near_ref, near_cross_ref, far_ref, far_cross_ref, out_ref):
    core, far_side, along = place_ref[0], 1 - place_ref[2], place_ref[3]
    share = near_ref.shape[1]

    def pair(j, carry):
        side, group, c, k = j // (4 * share), j // share % 4, j // (share // 2) % 2, j % (share // 2) * 2
        piece = (along + 4 - group) % 4
        rows = []
        for h in range(2):
            near = jnp.where(core == c, near_ref[piece, k + h].astype(f32), near_cross_ref[piece, k + h].astype(f32))
            far = jnp.where(core == c, far_ref[piece, k + h].astype(f32), far_cross_ref[piece, k + h].astype(f32))
            table = jnp.where(side == far_side, far, near)
            low, high = table[:, :LANES], table[:, LANES:]
            row = codes_ref[pl.ds(2 * j + h, 1), :]
            parts = []
            for t in range(row.shape[1] // LANES):
                code = jnp.broadcast_to(row[:, t * LANES : (t + 1) * LANES], (8, LANES))
                index = code & (LANES - 1)
                parts.append(
                    jnp.where(
                        code < LANES,
                        jnp.take_along_axis(low, index, axis=1, mode="promise_in_bounds"),
                        jnp.take_along_axis(high, index, axis=1, mode="promise_in_bounds"),
                    )
                )
            rows.append(jnp.concatenate(parts, axis=1))
        out_ref[pl.ds(pl.multiple_of(16 * j, 16), 16), :] = jnp.concatenate(rows, axis=0).astype(bf16)
        return carry

    lax.fori_loop(0, codes_ref.shape[0] // 2, pair, 0, unroll=8)


def local_logs(pack_ref, passages_ref):
    rows = []
    for b in range(2):
        tile = jnp.dot(query_rows(pack_ref, b * 8, 8), passages_ref[...], preferred_element_type=f32)
        peak = jnp.max(tile, axis=1, keepdims=True)
        total = jnp.sum(jnp.exp(tile - peak), axis=1, keepdims=True)
        row = as_row(peak + jnp.log(total))
        rows += [row[:, j * LANES : (j + 1) * LANES] for j in range(2)]
    return jnp.concatenate(rows, axis=0)


def own_scores_kernel(pack_ref, passages_ref, logs_ref):
    logs_ref[...] = local_logs(pack_ref, passages_ref)


def other_scores_kernel(pack_ref, passages_ref, own_logs_ref, stats_ref):
    logs = jnp.concatenate([own_logs_ref[...], local_logs(pack_ref, passages_ref)], axis=0)
    stats_ref[...] = jnp.broadcast_to(logs[None], stats_ref.shape)


def log_totals(core, stats_ref, h):
    peers = stats_ref.shape[0]
    same = (lax.broadcasted_iota(i32, (peers, LANES), 0) & 1) == core
    out = []
    for j in range(4):
        logs = jnp.where(same, stats_ref[:, 4 * h + j, :], stats_ref[:, 4 - 4 * h + j, :])
        peak = jnp.max(logs, axis=0, keepdims=True)
        out.append(peak + jnp.log(jnp.sum(jnp.exp(logs - peak), axis=0, keepdims=True)))
    return out


def weights_kernel(
    place_ref, stats_ref, own_ref, other_ref, passages_ref, other_sums_ref, own_sums_ref, grads_ref,
    high_ref, low_ref, turned_ref
):
    core, offset = place_ref[0], place_ref[1]
    half, passage_count = own_sums_ref.shape[0], passages_ref.shape[1]
    size = half // own_ref.shape[0]
    passages = passages_ref[...]
    spot = lax.broadcasted_iota(i32, (size, passage_count), 1) + offset
    for h, pack_ref, sums_ref in ((1, other_ref, other_sums_ref), (0, own_ref, own_sums_ref)):
        for t in range(turned_ref.shape[0] // LANES):
            columns = query_columns(pack_ref, t, 0, pack_ref.shape[0])
            turned_ref[t * LANES : (t + 1) * LANES, h * half : (h + 1) * half] = jnp.transpose(columns)
        totals = [as_column(row) for row in log_totals(core, stats_ref, h)]
        targets = target_columns(pack_ref)[:size].astype(i32)
        for b in range(half // BLOCK):
            tile = jnp.dot(query_rows(pack_ref, b * 8, 8), passages, preferred_element_type=f32)
            tile = jnp.exp(tile - jnp.concatenate(totals[2 * b : 2 * b + 2], axis=0))
            rows = slice(h * half + b * BLOCK, h * half + (b + 1) * BLOCK)
            pieces = []
            for c in range(BLOCK // size):
                place = b * BLOCK // size + c
                hits = jnp.where(targets[:, place : place + 1] == spot, 1.0, 0.0)
                pieces.append(tile[c * size : (c + 1) * size] - hits)
            weight = jnp.concatenate(pieces, axis=0)
            high = weight.astype(bf16)
            low = (weight - high.astype(f32)).astype(bf16)
            high_ref[rows] = high
            low_ref[rows] = low
            sums_ref[b * BLOCK : (b + 1) * BLOCK] = lax.dot_general(
                high, passages, ROWS_BY_ROWS, preferred_element_type=f32
            ) + lax.dot_general(low, passages, ROWS_BY_ROWS, preferred_element_type=f32)
    for n in range(passage_count // BLOCK):
        columns = slice(n * BLOCK, (n + 1) * BLOCK)
        grad = jnp.dot(turned_ref[...], high_ref[:, columns], preferred_element_type=f32) + jnp.dot(
            turned_ref[...], low_ref[:, columns], preferred_element_type=f32
        )
        grads_ref[:, columns] = grad.astype(bf16)


def codeword_sums(core, grads_ref, codes_ref, out_ref):
    word = lax.broadcasted_iota(i32, (64, codes_ref.shape[1]), 0)

    def two(j, carry):
        first = j // 3 * 12 + 6 * core + 2 * (j % 3)
        grads = grads_ref[pl.ds(pl.multiple_of(8 * first, 16), 16), :].astype(f32)
        sums = []
        for m in range(2):
            grad = grads[8 * m : 8 * m + 8]
            code = codes_ref[pl.ds(first + m, 1), :]
            high = code >> 6
            parts = jnp.concatenate([jnp.where(high == t, grad, 0.0) for t in range(4)], axis=0).astype(bf16)
            onehot = jnp.where((code & 63) == word, 1.0, 0.0).astype(bf16)
            sums.append(lax.dot_general(parts, onehot, ROWS_BY_ROWS, preferred_element_type=f32))
        sums = jnp.concatenate(sums, axis=1)
        for k in range(2):
            out_ref[j // 3, k, j % 3] = sums[16 * k : 16 * k + 16]
        return carry

    lax.fori_loop(0, codes_ref.shape[0] // 4, two, 0, unroll=24)


def codeword_kernel(place_ref, grads_ref, codes_ref, out_ref):
    codeword_sums(1 - place_ref[0], grads_ref, codes_ref, out_ref)


def put_query_words(chunk, out_ref, c):
    size, width = chunk.shape
    exponent = exponents(chunk)
    words = as_words(chunk, exponent)
    for t in range(width // LANES):
        out_ref[c, t * size : (t + 1) * size] = words[:, t * LANES : (t + 1) * LANES]
    return exponent


def take_query_words(words_ref, c, scale, width):
    size = scale.shape[0]
    words = [words_ref[c, t * size : (t + 1) * size] for t in range(width // LANES)]
    return jnp.concatenate([word.astype(i32).astype(f32) * scale for word in words], axis=1)


def send_kernel(place_ref, grads_ref, codes_ref, sums_ref, cross_ref, parts_ref, out_ref):
    peers = out_ref.shape[0]
    half, width = sums_ref.shape
    size = half // (2 * peers)
    for c in range(peers):
        rows = pl.ds(pl.multiple_of((1 - place_ref[4]) * (half // 2) + c * size, size), size)
        exponent = put_query_words(sums_ref[rows] + cross_ref[rows], out_ref, c)
        out_ref[c, width // LANES * size :] = exponent_rows(exponent)
    codeword_sums(place_ref[0], grads_ref, codes_ref, parts_ref)


def pack_kernel(place_ref, sums_ref, cross_ref, words_ref, parts_ref, out_ref):
    peers = out_ref.shape[0]
    half, width = sums_ref.shape
    size = half // (2 * peers)
    base = width // LANES * size
    totals = parts_ref[0]
    for c in range(1, parts_ref.shape[0]):
        totals = totals + parts_ref[c]
    totals = totals.reshape(-1, LANES)
    totals_exponent = exponents(totals)
    totals = as_words(totals, totals_exponent)
    for c in range(peers):
        rows = pl.ds(pl.multiple_of(place_ref[4] * (half // 2) + c * size, size), size)
        received = take_query_words(words_ref, c, scale_column(words_ref[c, base:], size), width)
        exponent = put_query_words(sums_ref[rows] + cross_ref[rows] + received, out_ref, c)
        out_ref[c, base : base + totals.shape[0]] = totals
        out_ref[c, base + totals.shape[0] :] = exponent_rows(jnp.concatenate([exponent, totals_exponent], axis=0))


def unpack_query_kernel(words_ref, query_ref):
    peers, length, _ = words_ref.shape
    size, width = query_ref.shape
    query = 0.0
    for c in range(peers):
        query = query + take_query_words(words_ref, c, scale_column(words_ref[c, length - 16 :], size), width)
    query_ref[...] = query.astype(bf16)


def unpack_sums_kernel(size, words_ref, sums_ref):
    peers, length, _ = words_ref.shape
    count = sums_ref.shape[0]
    start = length - 16 - count
    sums = 0.0
    for c in range(peers):
        scale = scale_column(words_ref[c, length - 16 :], size + count)[size:]
        sums = sums + words_ref[c, start : start + count].astype(i32).astype(f32) * scale
    sums_ref[...] = sums


def join_kernel(place_ref, own_ref, beside_ref, cross_ref, corner_ref, out_ref, all_ref):
    core, side = place_ref[0], place_ref[4]
    all_ref[2 * core + side] = own_ref[...]
    all_ref[2 * core + 1 - side] = beside_ref[...]
    all_ref[2 - 2 * core + side] = cross_ref[...]
    all_ref[2 - 2 * core + 1 - side] = corner_ref[...]
    for c in range(2):
        for j in range(3):
            rows = [all_ref[2 * c + t // 2, 16 * j + t % 2 * 8 : 16 * j + t % 2 * 8 + 8] for t in range(4)]
            for m in range(2):
                out_ref[6 * c + 2 * j + m] = jnp.concatenate([row[:, 64 * m : 64 * m + 64] for row in rows], axis=1)


IN_VMEM = pl.BlockSpec(memory_space=pltpu.VMEM)
ANYWHERE = pl.BlockSpec(memory_space=pl.ANY)
IN_SMEM = pl.BlockSpec(memory_space=pltpu.SMEM)


def call(kernel, shapes, args, flops, scratch=(), special=None, out_special=None, vmem=12):
    specs = [IN_VMEM] * len(args)
    for place, spec in (special or {}).items():
        specs[place] = spec
    many = isinstance(shapes, list)
    outs = [IN_VMEM] * (len(shapes) if many else 1)
    for place, spec in (out_special or {}).items():
        outs[place] = spec
    return pl.pallas_call(
        kernel,
        out_shape=shapes,
        in_specs=specs,
        out_specs=outs if many else outs[0],
        scratch_shapes=scratch,
        compiler_params=pltpu.CompilerParams(vmem_limit_bytes=vmem * 2**20),
        cost_estimate=pl.CostEstimate(flops=flops, bytes_accessed=2**16, transcendentals=0),
    )(*args)


def per_device(queries, codes, positives, codebook):
    swap = functools.partial(lax.ppermute, axis_name="core", perm=[(0, 1), (1, 0)])
    swap_x = functools.partial(lax.ppermute, axis_name="xl", perm=[(0, 1), (1, 0)])
    shape = jax.ShapeDtypeStruct
    own_codes = codes[0]
    subspaces, passage_count = own_codes.shape
    size, width = queries.shape[1:]
    chips = 16
    half = chips * size
    offset = lax.axis_index(("xl", "z", "core")) * passage_count
    axes = [lax.axis_index(name) for name in ("core", "xh", "y", "xl")]
    place = jnp.stack([axes[0], offset, *axes[1:]]).astype(i32)
    scalar = {0: IN_SMEM}
    length = width // LANES * size + 16
    own = call(
        spread_kernel,
        shape((chips, length, LANES), bf16),
        (queries[0], positives),
        10**6,
        scratch=[pltpu.VMEM((length, LANES), bf16), pltpu.SemaphoreType.DMA((chips,))],
        out_special={0: ANYWHERE},
        vmem=60,
    )
    share = call(
        share_kernel,
        shape((codebook.shape[0] // 2, *codebook.shape[1:]), bf16),
        (place, codebook),
        10**6,
        special=scalar,
    )
    near = [share] + [lax.ppermute(share, "y", [(i, (i + k) % 4) for i in range(4)]) for k in range(1, 4)]
    near = jnp.stack(near)
    far = lax.ppermute(near, "xh", [(0, 1), (1, 0)])
    own = lax.all_to_all(own, CHIP, 0, 0)
    passages = call(
        decode_kernel,
        shape((width, passage_count), bf16),
        (place, own_codes, near, swap(near), far, swap(far)),
        10**6,
        special=scalar,
    )
    own, passages = lax.optimization_barrier((own, passages))
    other = swap(own)
    own_logs = call(own_scores_kernel, shape((4, LANES), f32), (own, passages), 10**6)
    stats = call(other_scores_kernel, shape((32, 8, LANES), f32), (other, passages, own_logs), 10**6)
    stats = lax.all_to_all(stats, CHIP + ("core",), 0, 0, tiled=True)
    query_other, query_own, grads = call(
        weights_kernel,
        [shape((half, width), f32), shape((half, width), f32), shape((width, passage_count), bf16)],
        (place, stats, own, other, passages),
        10**6,
        scratch=[
            pltpu.VMEM((2 * half, passage_count), bf16),
            pltpu.VMEM((2 * half, passage_count), bf16),
            pltpu.VMEM((width, 2 * half), bf16),
        ],
        special=scalar,
        vmem=20,
    )
    query_cross = swap(query_other)

    sums_shape = shape((8, 2, subspaces // 32, 16, LANES), f32)
    parts_cross = swap(call(codeword_kernel, sums_shape, (place, grads, own_codes), 10**6, special=scalar))
    parts, words = call(
        send_kernel,
        [sums_shape, shape((chips // 2, length, LANES), i16)],
        (place, grads, own_codes, query_own, query_cross),
        10**6,
        special=scalar,
    )
    parts = parts + parts_cross
    parts, words = lax.optimization_barrier((parts, words))
    words = swap_x(words)
    parts = lax.all_to_all(parts.reshape(16, subspaces // 32, 16, LANES), SUB + ("xl",), 0, 0)
    count = subspaces // 32 * 16
    words = call(
        pack_kernel,
        shape((chips // 2, length + count, LANES), i16),
        (place, query_own, query_cross, words, parts),
        10**6,
        special=scalar,
    )
    words = lax.all_to_all(words, "z", 0, 0)
    sums = call(functools.partial(unpack_sums_kernel, size), shape((count, LANES), f32), (words,), 10**6)
    beside = swap_x(sums)
    corner = lax.ppermute(sums, ("xl", "core"), [(i, 3 - i) for i in range(4)])
    cross = swap(sums)
    query_grad = call(unpack_query_kernel, shape((size, width), bf16), (words,), 10**6)
    codeword_grad = call(
        join_kernel,
        shape((subspaces // 8, 8, 2 * LANES), f32),
        (place, sums, beside, cross, corner),
        10**6,
        scratch=[pltpu.VMEM((4, count, LANES), f32)],
        special=scalar,
    )
    return query_grad[None], codeword_grad


def solution(mesh):
    split = Mesh(mesh.devices.reshape(2, 8, 2, 2, 4), ("xl", "z", "core", "xh", "y"))
    blk = ("xl", "z", "core")
    return jax.shard_map(
        per_device,
        mesh=split,
        in_specs=(P(SUB, blk, None), P(SUB, None, blk), P(SUB, blk), P(SUB, None, None)),
        out_specs=(P(SUB, blk, None), P(SUB, None, None)),
        check_vma=False,
    )
```

```python
import functools

import jax
import jax.numpy as jnp
from jax import lax
from jax.experimental import pallas as pl
from jax.experimental.pallas import tpu as pltpu
from jax.sharding import Mesh, PartitionSpec as P

f32 = jnp.float32
bf16 = jnp.bfloat16
i32 = jnp.int32
i16 = jnp.int16
LANES = 128
BLOCK = 256
CHIP = ("xl", "z")
SUB = ("xh", "y")
ROWS_BY_ROWS = (((1,), (1,)), ((), ()))


def as_column(row):
    return jnp.transpose(jnp.broadcast_to(row, (LANES, row.shape[1])))[:, :1]


def as_row(column):
    return jnp.transpose(jnp.broadcast_to(column, (column.shape[0], LANES)))[:1]


def exponents(rows):
    peak = jnp.maximum(jnp.max(jnp.abs(rows), axis=1, keepdims=True), 2.0**-100)
    return jnp.ceil(jnp.log2(peak * (1.0 / 32767.0)))


def as_words(rows, exponent):
    scaled = jnp.round(rows * jnp.exp2(-exponent))
    return jnp.clip(scaled, -32767.0, 32767.0).astype(i32).astype(i16)


def exponent_tails(query, sums=None):
    size = query[0].shape[0]
    lane = lax.broadcasted_iota(i32, (size, LANES), 1)
    block = jnp.zeros((size, LANES), f32)
    for c, exponent in enumerate(query):
        block = jnp.where(lane == c, exponent, block)
    parts = [block] if sums is None else [block, jnp.broadcast_to(sums, (sums.shape[0], LANES))]
    parts.append(jnp.zeros((LANES - sum(part.shape[0] for part in parts), LANES), f32))
    turned = jnp.transpose(jnp.concatenate(parts, axis=0))
    return [jnp.broadcast_to(turned[c : c + 1], (16, LANES)).astype(i32).astype(i16) for c in range(len(query))]


def scale_columns(words_ref):
    peers, length, _ = words_ref.shape
    rows = [words_ref[c, length - 16 :].astype(i32).astype(f32)[:1] for c in range(peers)]
    rows.append(jnp.zeros((LANES - peers, LANES), f32))
    return jnp.exp2(jnp.transpose(jnp.concatenate(rows, axis=0)))


def spread_kernel(queries_ref, positives_ref, out_ref, block_ref, sems):
    size, width = queries_ref.shape
    target = jnp.concatenate([positives_ref[...], jnp.zeros((1, LANES - size), i32)], axis=1)
    tail = jnp.concatenate([target // LANES, target % LANES, jnp.zeros((14, LANES), i32)], axis=0)
    for t in range(width // LANES):
        block_ref[t * size : (t + 1) * size] = queries_ref[:, t * LANES : (t + 1) * LANES]
    block_ref[width // LANES * size :] = tail.astype(f32).astype(bf16)
    sends = [pltpu.make_async_copy(block_ref, out_ref.at[c], sems.at[c]) for c in range(out_ref.shape[0])]
    for send in sends:
        send.start()
    for send in sends:
        send.wait()


def share_kernel(place_ref, book_ref, share_ref):
    count = share_ref.shape[0]
    share_ref[...] = book_ref[pl.ds(place_ref[0] * count, count)]


def query_columns(pack_ref, t, first, count):
    size = (pack_ref.shape[1] - 16) // 6
    return pack_ref[first : first + count, t * size : (t + 1) * size, :].reshape(count * size, LANES)


def query_rows(pack_ref, first, count):
    return jnp.concatenate([query_columns(pack_ref, t, first, count) for t in range(6)], axis=1)


def target_columns(pack_ref):
    chips, length, _ = pack_ref.shape
    tail = pack_ref[:, length - 16 :, :].astype(f32)
    target = tail[:, 0, :] * LANES + tail[:, 1, :]
    target = jnp.concatenate([target, jnp.zeros((LANES - chips, LANES), f32)], axis=0)
    return jnp.transpose(target)


def decode_kernel(place_ref, codes_ref, near_ref, near_cross_ref, far_ref, far_cross_ref, out_ref):
    core, far_side, along = place_ref[0], 1 - place_ref[2], place_ref[3]
    share = near_ref.shape[1]

    def pair(j, carry):
        side, group, c, k = j // (4 * share), j // share % 4, j // (share // 2) % 2, j % (share // 2) * 2
        piece = (along + 4 - group) % 4
        rows = []
        for h in range(2):
            near = jnp.where(core == c, near_ref[piece, k + h].astype(f32), near_cross_ref[piece, k + h].astype(f32))
            far = jnp.where(core == c, far_ref[piece, k + h].astype(f32), far_cross_ref[piece, k + h].astype(f32))
            table = jnp.where(side == far_side, far, near)
            low, high = table[:, :LANES], table[:, LANES:]
            row = codes_ref[pl.ds(2 * j + h, 1), :]
            parts = []
            for t in range(row.shape[1] // LANES):
                code = jnp.broadcast_to(row[:, t * LANES : (t + 1) * LANES], (8, LANES))
                index = code & (LANES - 1)
                parts.append(
                    jnp.where(
                        code < LANES,
                        jnp.take_along_axis(low, index, axis=1, mode="promise_in_bounds"),
                        jnp.take_along_axis(high, index, axis=1, mode="promise_in_bounds"),
                    )
                )
            rows.append(jnp.concatenate(parts, axis=1))
        out_ref[pl.ds(pl.multiple_of(16 * j, 16), 16), :] = jnp.concatenate(rows, axis=0).astype(bf16)
        return carry

    lax.fori_loop(0, codes_ref.shape[0] // 2, pair, 0, unroll=8)


def local_logs(pack_ref, passages_ref):
    rows = []
    for b in range(2):
        tile = jnp.dot(query_rows(pack_ref, b * 8, 8), passages_ref[...], preferred_element_type=f32)
        peak = jnp.max(tile, axis=1, keepdims=True)
        total = jnp.sum(jnp.exp(tile - peak), axis=1, keepdims=True)
        row = as_row(peak + jnp.log(total))
        rows += [row[:, j * LANES : (j + 1) * LANES] for j in range(2)]
    return jnp.concatenate(rows, axis=0)


def own_scores_kernel(pack_ref, passages_ref, logs_ref):
    logs_ref[...] = local_logs(pack_ref, passages_ref)


def other_scores_kernel(pack_ref, passages_ref, own_logs_ref, stats_ref):
    logs = jnp.concatenate([own_logs_ref[...], local_logs(pack_ref, passages_ref)], axis=0)
    stats_ref[...] = jnp.broadcast_to(logs[None], stats_ref.shape)


def log_totals(core, stats_ref, h):
    peers = stats_ref.shape[0]
    same = (lax.broadcasted_iota(i32, (peers, LANES), 0) & 1) == core
    out = []
    for j in range(4):
        logs = jnp.where(same, stats_ref[:, 4 * h + j, :], stats_ref[:, 4 - 4 * h + j, :])
        peak = jnp.max(logs, axis=0, keepdims=True)
        out.append(peak + jnp.log(jnp.sum(jnp.exp(logs - peak), axis=0, keepdims=True)))
    return out


def weights_kernel(
    place_ref, stats_ref, own_ref, other_ref, passages_ref, other_sums_ref, own_sums_ref, grads_ref,
    high_ref, low_ref, turned_ref
):
    core, offset = place_ref[0], place_ref[1]
    half, passage_count = own_sums_ref.shape[0], passages_ref.shape[1]
    size = half // own_ref.shape[0]
    passages = passages_ref[...]
    spot = lax.broadcasted_iota(i32, (size, passage_count), 1) + offset
    for h, pack_ref, sums_ref in ((1, other_ref, other_sums_ref), (0, own_ref, own_sums_ref)):
        for t in range(turned_ref.shape[0] // LANES):
            columns = query_columns(pack_ref, t, 0, pack_ref.shape[0])
            turned_ref[t * LANES : (t + 1) * LANES, h * half : (h + 1) * half] = jnp.transpose(columns)
        totals = [as_column(row) for row in log_totals(core, stats_ref, h)]
        targets = target_columns(pack_ref)[:size].astype(i32)
        for b in range(half // BLOCK):
            tile = jnp.dot(query_rows(pack_ref, b * 8, 8), passages, preferred_element_type=f32)
            tile = jnp.exp(tile - jnp.concatenate(totals[2 * b : 2 * b + 2], axis=0))
            rows = slice(h * half + b * BLOCK, h * half + (b + 1) * BLOCK)
            pieces = []
            for c in range(BLOCK // size):
                place = b * BLOCK // size + c
                hits = jnp.where(targets[:, place : place + 1] == spot, 1.0, 0.0)
                pieces.append(tile[c * size : (c + 1) * size] - hits)
            weight = jnp.concatenate(pieces, axis=0)
            high = weight.astype(bf16)
            low = (weight - high.astype(f32)).astype(bf16)
            high_ref[rows] = high
            low_ref[rows] = low
            sums_ref[b * BLOCK : (b + 1) * BLOCK] = lax.dot_general(
                high, passages, ROWS_BY_ROWS, preferred_element_type=f32
            ) + lax.dot_general(low, passages, ROWS_BY_ROWS, preferred_element_type=f32)
    for n in range(passage_count // BLOCK):
        columns = slice(n * BLOCK, (n + 1) * BLOCK)
        grad = jnp.dot(turned_ref[...], high_ref[:, columns], preferred_element_type=f32) + jnp.dot(
            turned_ref[...], low_ref[:, columns], preferred_element_type=f32
        )
        grads_ref[:, columns] = grad.astype(bf16)


def codeword_sums(core, grads_ref, codes_ref, out_ref):
    word = lax.broadcasted_iota(i32, (64, codes_ref.shape[1]), 0)

    def two(j, carry):
        first = j // 3 * 12 + 6 * core + 2 * (j % 3)
        grads = grads_ref[pl.ds(pl.multiple_of(8 * first, 16), 16), :].astype(f32)
        sums = []
        for m in range(2):
            grad = grads[8 * m : 8 * m + 8]
            code = codes_ref[pl.ds(first + m, 1), :]
            high = code >> 6
            parts = jnp.concatenate([jnp.where(high == t, grad, 0.0) for t in range(4)], axis=0).astype(bf16)
            onehot = jnp.where((code & 63) == word, 1.0, 0.0).astype(bf16)
            sums.append(lax.dot_general(parts, onehot, ROWS_BY_ROWS, preferred_element_type=f32))
        sums = jnp.concatenate(sums, axis=1)
        for k in range(2):
            out_ref[j // 3, k, j % 3] = sums[16 * k : 16 * k + 16]
        return carry

    lax.fori_loop(0, codes_ref.shape[0] // 4, two, 0, unroll=24)


def codeword_kernel(place_ref, grads_ref, codes_ref, out_ref):
    codeword_sums(1 - place_ref[0], grads_ref, codes_ref, out_ref)


def put_query_words(chunk, out_ref, c):
    size, width = chunk.shape
    exponent = exponents(chunk)
    words = as_words(chunk, exponent)
    for t in range(width // LANES):
        out_ref[c, t * size : (t + 1) * size] = words[:, t * LANES : (t + 1) * LANES]
    return exponent


def take_query_words(words_ref, c, scale, width):
    size = scale.shape[0]
    words = [words_ref[c, t * size : (t + 1) * size] for t in range(width // LANES)]
    return jnp.concatenate([word.astype(i32).astype(f32) * scale for word in words], axis=1)


def send_kernel(place_ref, grads_ref, codes_ref, sums_ref, cross_ref, parts_ref, out_ref):
    peers = out_ref.shape[0]
    half, width = sums_ref.shape
    size = half // (2 * peers)
    query = []
    for c in range(peers):
        rows = pl.ds(pl.multiple_of((1 - place_ref[4]) * (half // 2) + c * size, size), size)
        query.append(put_query_words(sums_ref[rows] + cross_ref[rows], out_ref, c))
    for c, tail in enumerate(exponent_tails(query)):
        out_ref[c, width // LANES * size :] = tail
    codeword_sums(place_ref[0], grads_ref, codes_ref, parts_ref)


def pack_kernel(place_ref, sums_ref, cross_ref, words_ref, parts_ref, out_ref):
    peers = out_ref.shape[0]
    half, width = sums_ref.shape
    size = half // (2 * peers)
    base = width // LANES * size
    totals = parts_ref[0]
    for c in range(1, parts_ref.shape[0]):
        totals = totals + parts_ref[c]
    totals = totals.reshape(-1, LANES)
    totals_exponent = exponents(totals)
    totals = as_words(totals, totals_exponent)
    scales = scale_columns(words_ref)
    query = []
    for c in range(peers):
        rows = pl.ds(pl.multiple_of(place_ref[4] * (half // 2) + c * size, size), size)
        received = take_query_words(words_ref, c, scales[:size, c : c + 1], width)
        query.append(put_query_words(sums_ref[rows] + cross_ref[rows] + received, out_ref, c))
        out_ref[c, base : base + totals.shape[0]] = totals
    for c, tail in enumerate(exponent_tails(query, totals_exponent)):
        out_ref[c, base + totals.shape[0] :] = tail


def unpack_query_kernel(words_ref, query_ref):
    peers = words_ref.shape[0]
    size, width = query_ref.shape
    scales = scale_columns(words_ref)
    query = 0.0
    for c in range(peers):
        query = query + take_query_words(words_ref, c, scales[:size, c : c + 1], width)
    query_ref[...] = query.astype(bf16)


def unpack_sums_kernel(size, words_ref, sums_ref):
    peers, length, _ = words_ref.shape
    count = sums_ref.shape[0]
    start = length - 16 - count
    scales = scale_columns(words_ref)
    sums = 0.0
    for c in range(peers):
        scale = scales[size : size + count, c : c + 1]
        sums = sums + words_ref[c, start : start + count].astype(i32).astype(f32) * scale
    sums_ref[...] = sums


def join_kernel(place_ref, own_ref, beside_ref, cross_ref, corner_ref, out_ref, all_ref):
    core, side = place_ref[0], place_ref[4]
    all_ref[2 * core + side] = own_ref[...]
    all_ref[2 * core + 1 - side] = beside_ref[...]
    all_ref[2 - 2 * core + side] = cross_ref[...]
    all_ref[2 - 2 * core + 1 - side] = corner_ref[...]
    for c in range(2):
        for j in range(3):
            rows = [all_ref[2 * c + t // 2, 16 * j + t % 2 * 8 : 16 * j + t % 2 * 8 + 8] for t in range(4)]
            for m in range(2):
                out_ref[6 * c + 2 * j + m] = jnp.concatenate([row[:, 64 * m : 64 * m + 64] for row in rows], axis=1)


IN_VMEM = pl.BlockSpec(memory_space=pltpu.VMEM)
ANYWHERE = pl.BlockSpec(memory_space=pl.ANY)
IN_SMEM = pl.BlockSpec(memory_space=pltpu.SMEM)


def call(kernel, shapes, args, flops, scratch=(), special=None, out_special=None, vmem=12):
    specs = [IN_VMEM] * len(args)
    for place, spec in (special or {}).items():
        specs[place] = spec
    many = isinstance(shapes, list)
    outs = [IN_VMEM] * (len(shapes) if many else 1)
    for place, spec in (out_special or {}).items():
        outs[place] = spec
    return pl.pallas_call(
        kernel,
        out_shape=shapes,
        in_specs=specs,
        out_specs=outs if many else outs[0],
        scratch_shapes=scratch,
        compiler_params=pltpu.CompilerParams(vmem_limit_bytes=vmem * 2**20),
        cost_estimate=pl.CostEstimate(flops=flops, bytes_accessed=2**16, transcendentals=0),
    )(*args)


def per_device(queries, codes, positives, codebook):
    swap = functools.partial(lax.ppermute, axis_name="core", perm=[(0, 1), (1, 0)])
    swap_x = functools.partial(lax.ppermute, axis_name="xl", perm=[(0, 1), (1, 0)])
    shape = jax.ShapeDtypeStruct
    own_codes = codes[0]
    subspaces, passage_count = own_codes.shape
    size, width = queries.shape[1:]
    chips = 16
    half = chips * size
    offset = lax.axis_index(("xl", "z", "core")) * passage_count
    axes = [lax.axis_index(name) for name in ("core", "xh", "y", "xl")]
    place = jnp.stack([axes[0], offset, *axes[1:]]).astype(i32)
    scalar = {0: IN_SMEM}
    length = width // LANES * size + 16
    own = call(
        spread_kernel,
        shape((chips, length, LANES), bf16),
        (queries[0], positives),
        10**6,
        scratch=[pltpu.VMEM((length, LANES), bf16), pltpu.SemaphoreType.DMA((chips,))],
        out_special={0: ANYWHERE},
        vmem=60,
    )
    share = call(
        share_kernel,
        shape((codebook.shape[0] // 2, *codebook.shape[1:]), bf16),
        (place, codebook),
        10**6,
        special=scalar,
    )
    near = [share] + [lax.ppermute(share, "y", [(i, (i + k) % 4) for i in range(4)]) for k in range(1, 4)]
    near = jnp.stack(near)
    far = lax.ppermute(near, "xh", [(0, 1), (1, 0)])
    own = lax.all_to_all(own, CHIP, 0, 0)
    passages = call(
        decode_kernel,
        shape((width, passage_count), bf16),
        (place, own_codes, near, swap(near), far, swap(far)),
        10**6,
        special=scalar,
    )
    own, passages = lax.optimization_barrier((own, passages))
    other = swap(own)
    own_logs = call(own_scores_kernel, shape((4, LANES), f32), (own, passages), 10**6)
    stats = call(other_scores_kernel, shape((32, 8, LANES), f32), (other, passages, own_logs), 10**6)
    stats = lax.all_to_all(stats, CHIP + ("core",), 0, 0, tiled=True)
    query_other, query_own, grads = call(
        weights_kernel,
        [shape((half, width), f32), shape((half, width), f32), shape((width, passage_count), bf16)],
        (place, stats, own, other, passages),
        10**6,
        scratch=[
            pltpu.VMEM((2 * half, passage_count), bf16),
            pltpu.VMEM((2 * half, passage_count), bf16),
            pltpu.VMEM((width, 2 * half), bf16),
        ],
        special=scalar,
        vmem=20,
    )
    query_cross = swap(query_other)

    sums_shape = shape((8, 2, subspaces // 32, 16, LANES), f32)
    parts_cross = swap(call(codeword_kernel, sums_shape, (place, grads, own_codes), 10**6, special=scalar))
    parts, words = call(
        send_kernel,
        [sums_shape, shape((chips // 2, length, LANES), i16)],
        (place, grads, own_codes, query_own, query_cross),
        10**6,
        special=scalar,
    )
    parts = parts + parts_cross
    parts, words = lax.optimization_barrier((parts, words))
    words = swap_x(words)
    parts = lax.all_to_all(parts.reshape(16, subspaces // 32, 16, LANES), SUB + ("xl",), 0, 0)
    count = subspaces // 32 * 16
    words = call(
        pack_kernel,
        shape((chips // 2, length + count, LANES), i16),
        (place, query_own, query_cross, words, parts),
        10**6,
        special=scalar,
    )
    words = lax.all_to_all(words, "z", 0, 0)
    sums = call(functools.partial(unpack_sums_kernel, size), shape((count, LANES), f32), (words,), 10**6)
    beside = swap_x(sums)
    corner = lax.ppermute(sums, ("xl", "core"), [(i, 3 - i) for i in range(4)])
    cross = swap(sums)
    query_grad = call(unpack_query_kernel, shape((size, width), bf16), (words,), 10**6)
    codeword_grad = call(
        join_kernel,
        shape((subspaces // 8, 8, 2 * LANES), f32),
        (place, sums, beside, cross, corner),
        10**6,
        scratch=[pltpu.VMEM((4, count, LANES), f32)],
        special=scalar,
    )
    return query_grad[None], codeword_grad


def solution(mesh):
    split = Mesh(mesh.devices.reshape(2, 8, 2, 2, 4), ("xl", "z", "core", "xh", "y"))
    blk = ("xl", "z", "core")
    return jax.shard_map(
        per_device,
        mesh=split,
        in_specs=(P(SUB, blk, None), P(SUB, None, blk), P(SUB, blk), P(SUB, None, None)),
        out_specs=(P(SUB, blk, None), P(SUB, None, None)),
        check_vma=False,
    )
```

```python
import functools

import jax
import jax.numpy as jnp
from jax import lax
from jax.experimental import pallas as pl
from jax.experimental.pallas import tpu as pltpu
from jax.sharding import Mesh, PartitionSpec as P

f32 = jnp.float32
bf16 = jnp.bfloat16
i32 = jnp.int32
i16 = jnp.int16
LANES = 128
BLOCK = 256
CHIP = ("xl", "z")
SUB = ("xh", "y")
ROWS_BY_ROWS = (((1,), (1,)), ((), ()))


def exponents(rows):
    peak = jnp.maximum(jnp.max(jnp.abs(rows), axis=1, keepdims=True), 2.0**-100)
    return jnp.ceil(jnp.log2(peak * (1.0 / 32767.0)))


def as_words(rows, exponent):
    scaled = jnp.round(rows * jnp.exp2(-exponent))
    return jnp.clip(scaled, -32767.0, 32767.0).astype(i32).astype(i16)


def exponent_tails(query, sums=None):
    size = query[0].shape[0]
    lane = lax.broadcasted_iota(i32, (size, LANES), 1)
    block = jnp.zeros((size, LANES), f32)
    for c, exponent in enumerate(query):
        block = jnp.where(lane == c, exponent, block)
    parts = [block] if sums is None else [block, jnp.broadcast_to(sums, (sums.shape[0], LANES))]
    parts.append(jnp.zeros((LANES - sum(part.shape[0] for part in parts), LANES), f32))
    turned = jnp.transpose(jnp.concatenate(parts, axis=0))
    return [jnp.broadcast_to(turned[c : c + 1], (16, LANES)).astype(i32).astype(i16) for c in range(len(query))]


def scale_columns(words_ref):
    peers, length, _ = words_ref.shape
    rows = [words_ref[c, length - 16 :].astype(i32).astype(f32)[:1] for c in range(peers)]
    rows.append(jnp.zeros((LANES - peers, LANES), f32))
    return jnp.exp2(jnp.transpose(jnp.concatenate(rows, axis=0)))


def spread_kernel(queries_ref, positives_ref, out_ref, block_ref, sems):
    size, width = queries_ref.shape
    target = jnp.concatenate([positives_ref[...], jnp.zeros((1, LANES - size), i32)], axis=1)
    tail = jnp.concatenate([target // LANES, target % LANES, jnp.zeros((14, LANES), i32)], axis=0)
    for t in range(width // LANES):
        block_ref[t * size : (t + 1) * size] = queries_ref[:, t * LANES : (t + 1) * LANES]
    block_ref[width // LANES * size :] = tail.astype(f32).astype(bf16)
    sends = [pltpu.make_async_copy(block_ref, out_ref.at[c], sems.at[c]) for c in range(out_ref.shape[0])]
    for send in sends:
        send.start()
    for send in sends:
        send.wait()


def share_kernel(place_ref, book_ref, share_ref):
    count = share_ref.shape[0]
    share_ref[...] = book_ref[pl.ds(place_ref[0] * count, count)]


def query_columns(pack_ref, t, first, count):
    size = (pack_ref.shape[1] - 16) // 6
    return pack_ref[first : first + count, t * size : (t + 1) * size, :].reshape(count * size, LANES)


def query_rows(pack_ref, first, count):
    return jnp.concatenate([query_columns(pack_ref, t, first, count) for t in range(6)], axis=1)


def target_columns(packs):
    parts = []
    for pack_ref in packs:
        length = pack_ref.shape[1]
        tail = pack_ref[:, length - 16 :, :].astype(f32)
        parts.append(tail[:, 0, :] * LANES + tail[:, 1, :])
    parts.append(jnp.zeros((LANES - sum(part.shape[0] for part in parts), LANES), f32))
    return jnp.transpose(jnp.concatenate(parts, axis=0))


def decode_kernel(place_ref, codes_ref, near_ref, near_cross_ref, far_ref, far_cross_ref, out_ref):
    core, far_side, along = place_ref[0], 1 - place_ref[2], place_ref[3]
    share = near_ref.shape[1]

    def pair(j, carry):
        side, group, c, k = j // (4 * share), j // share % 4, j // (share // 2) % 2, j % (share // 2) * 2
        piece = (along + 4 - group) % 4
        rows = []
        for h in range(2):
            near = jnp.where(core == c, near_ref[piece, k + h].astype(f32), near_cross_ref[piece, k + h].astype(f32))
            far = jnp.where(core == c, far_ref[piece, k + h].astype(f32), far_cross_ref[piece, k + h].astype(f32))
            table = jnp.where(side == far_side, far, near)
            low, high = table[:, :LANES], table[:, LANES:]
            row = codes_ref[pl.ds(2 * j + h, 1), :]
            parts = []
            for t in range(row.shape[1] // LANES):
                code = jnp.broadcast_to(row[:, t * LANES : (t + 1) * LANES], (8, LANES))
                index = code & (LANES - 1)
                parts.append(
                    jnp.where(
                        code < LANES,
                        jnp.take_along_axis(low, index, axis=1, mode="promise_in_bounds"),
                        jnp.take_along_axis(high, index, axis=1, mode="promise_in_bounds"),
                    )
                )
            rows.append(jnp.concatenate(parts, axis=1))
        out_ref[pl.ds(pl.multiple_of(16 * j, 16), 16), :] = jnp.concatenate(rows, axis=0).astype(bf16)
        return carry

    lax.fori_loop(0, codes_ref.shape[0] // 2, pair, 0, unroll=8)


def local_logs(pack_ref, passages_ref):
    lane = lax.broadcasted_iota(i32, (LANES, LANES), 1)
    block = jnp.zeros((LANES, LANES), f32)
    for b in range(2):
        tile = jnp.dot(query_rows(pack_ref, b * 8, 8), passages_ref[...], preferred_element_type=f32)
        peak = jnp.max(tile, axis=1, keepdims=True)
        logs = peak + jnp.log(jnp.sum(jnp.exp(tile - peak), axis=1, keepdims=True))
        for j in range(2):
            block = jnp.where(lane == 2 * b + j, logs[j * LANES : (j + 1) * LANES], block)
    return jnp.transpose(block)[:4]


def own_scores_kernel(pack_ref, passages_ref, logs_ref):
    logs_ref[...] = local_logs(pack_ref, passages_ref)


def other_scores_kernel(pack_ref, passages_ref, own_logs_ref, stats_ref):
    logs = jnp.concatenate([own_logs_ref[...], local_logs(pack_ref, passages_ref)], axis=0)
    stats_ref[...] = jnp.broadcast_to(logs[None], stats_ref.shape)


def log_totals(core, stats_ref, h):
    peers = stats_ref.shape[0]
    same = (lax.broadcasted_iota(i32, (peers, LANES), 0) & 1) == core
    out = []
    for j in range(4):
        logs = jnp.where(same, stats_ref[:, 4 * h + j, :], stats_ref[:, 4 - 4 * h + j, :])
        peak = jnp.max(logs, axis=0, keepdims=True)
        out.append(peak + jnp.log(jnp.sum(jnp.exp(logs - peak), axis=0, keepdims=True)))
    return out


def weights_kernel(
    place_ref, stats_ref, own_ref, other_ref, passages_ref, other_sums_ref, own_sums_ref, grads_ref,
    high_ref, low_ref, turned_ref
):
    core, offset = place_ref[0], place_ref[1]
    half, passage_count = own_sums_ref.shape[0], passages_ref.shape[1]
    size = half // own_ref.shape[0]
    passages = passages_ref[...]
    spot = lax.broadcasted_iota(i32, (size, passage_count), 1) + offset
    targets = target_columns((own_ref, other_ref))[:size].astype(i32)
    logs = log_totals(core, stats_ref, 0) + log_totals(core, stats_ref, 1)
    all_totals = jnp.transpose(jnp.concatenate([*logs, jnp.zeros((LANES - 8, LANES), f32)], axis=0))
    for h, pack_ref, sums_ref in ((1, other_ref, other_sums_ref), (0, own_ref, own_sums_ref)):
        for t in range(turned_ref.shape[0] // LANES):
            columns = query_columns(pack_ref, t, 0, pack_ref.shape[0])
            turned_ref[t * LANES : (t + 1) * LANES, h * half : (h + 1) * half] = jnp.transpose(columns)
        totals = [all_totals[:, 4 * h + j : 4 * h + j + 1] for j in range(4)]
        for b in range(half // BLOCK):
            tile = jnp.dot(query_rows(pack_ref, b * 8, 8), passages, preferred_element_type=f32)
            tile = jnp.exp(tile - jnp.concatenate(totals[2 * b : 2 * b + 2], axis=0))
            rows = slice(h * half + b * BLOCK, h * half + (b + 1) * BLOCK)
            pieces = []
            for c in range(BLOCK // size):
                place = (h * half + b * BLOCK) // size + c
                hits = jnp.where(targets[:, place : place + 1] == spot, 1.0, 0.0)
                pieces.append(tile[c * size : (c + 1) * size] - hits)
            weight = jnp.concatenate(pieces, axis=0)
            high = weight.astype(bf16)
            low = (weight - high.astype(f32)).astype(bf16)
            high_ref[rows] = high
            low_ref[rows] = low
            sums_ref[b * BLOCK : (b + 1) * BLOCK] = lax.dot_general(
                high, passages, ROWS_BY_ROWS, preferred_element_type=f32
            ) + lax.dot_general(low, passages, ROWS_BY_ROWS, preferred_element_type=f32)
    for n in range(passage_count // BLOCK):
        columns = slice(n * BLOCK, (n + 1) * BLOCK)
        grad = jnp.dot(turned_ref[...], high_ref[:, columns], preferred_element_type=f32) + jnp.dot(
            turned_ref[...], low_ref[:, columns], preferred_element_type=f32
        )
        grads_ref[:, columns] = grad.astype(bf16)


def codeword_sums(core, grads_ref, codes_ref, out_ref):
    word = lax.broadcasted_iota(i32, (64, codes_ref.shape[1]), 0)

    def two(j, carry):
        first = j // 3 * 12 + 6 * core + 2 * (j % 3)
        grads = grads_ref[pl.ds(pl.multiple_of(8 * first, 16), 16), :].astype(f32)
        sums = []
        for m in range(2):
            grad = grads[8 * m : 8 * m + 8]
            code = codes_ref[pl.ds(first + m, 1), :]
            high = code >> 6
            parts = jnp.concatenate([jnp.where(high == t, grad, 0.0) for t in range(4)], axis=0).astype(bf16)
            onehot = jnp.where((code & 63) == word, 1.0, 0.0).astype(bf16)
            sums.append(lax.dot_general(parts, onehot, ROWS_BY_ROWS, preferred_element_type=f32))
        sums = jnp.concatenate(sums, axis=1)
        for k in range(2):
            out_ref[j // 3, k, j % 3] = sums[16 * k : 16 * k + 16]
        return carry

    lax.fori_loop(0, codes_ref.shape[0] // 4, two, 0, unroll=24)


def codeword_kernel(place_ref, grads_ref, codes_ref, out_ref):
    codeword_sums(1 - place_ref[0], grads_ref, codes_ref, out_ref)


def put_query_words(chunk, out_ref, c):
    size, width = chunk.shape
    exponent = exponents(chunk)
    words = as_words(chunk, exponent)
    for t in range(width // LANES):
        out_ref[c, t * size : (t + 1) * size] = words[:, t * LANES : (t + 1) * LANES]
    return exponent


def take_query_words(words_ref, c, scale, width):
    size = scale.shape[0]
    words = [words_ref[c, t * size : (t + 1) * size] for t in range(width // LANES)]
    return jnp.concatenate([word.astype(i32).astype(f32) * scale for word in words], axis=1)


def send_kernel(place_ref, grads_ref, codes_ref, sums_ref, cross_ref, parts_ref, out_ref):
    peers = out_ref.shape[0]
    half, width = sums_ref.shape
    size = half // (2 * peers)
    query = []
    for c in range(peers):
        rows = pl.ds(pl.multiple_of((1 - place_ref[4]) * (half // 2) + c * size, size), size)
        query.append(put_query_words(sums_ref[rows] + cross_ref[rows], out_ref, c))
    for c, tail in enumerate(exponent_tails(query)):
        out_ref[c, width // LANES * size :] = tail
    codeword_sums(place_ref[0], grads_ref, codes_ref, parts_ref)


def pack_kernel(place_ref, sums_ref, cross_ref, words_ref, parts_ref, out_ref):
    peers = out_ref.shape[0]
    half, width = sums_ref.shape
    size = half // (2 * peers)
    base = width // LANES * size
    totals = parts_ref[0]
    for c in range(1, parts_ref.shape[0]):
        totals = totals + parts_ref[c]
    totals = totals.reshape(-1, LANES)
    totals_exponent = exponents(totals)
    totals = as_words(totals, totals_exponent)
    scales = scale_columns(words_ref)
    query = []
    for c in range(peers):
        rows = pl.ds(pl.multiple_of(place_ref[4] * (half // 2) + c * size, size), size)
        received = take_query_words(words_ref, c, scales[:size, c : c + 1], width)
        query.append(put_query_words(sums_ref[rows] + cross_ref[rows] + received, out_ref, c))
        out_ref[c, base : base + totals.shape[0]] = totals
    for c, tail in enumerate(exponent_tails(query, totals_exponent)):
        out_ref[c, base + totals.shape[0] :] = tail


def unpack_query_kernel(words_ref, query_ref):
    peers = words_ref.shape[0]
    size, width = query_ref.shape
    scales = scale_columns(words_ref)
    query = 0.0
    for c in range(peers):
        query = query + take_query_words(words_ref, c, scales[:size, c : c + 1], width)
    query_ref[...] = query.astype(bf16)


def unpack_sums_kernel(size, words_ref, sums_ref):
    peers, length, _ = words_ref.shape
    count = sums_ref.shape[0]
    start = length - 16 - count
    scales = scale_columns(words_ref)
    sums = 0.0
    for c in range(peers):
        scale = scales[size : size + count, c : c + 1]
        sums = sums + words_ref[c, start : start + count].astype(i32).astype(f32) * scale
    sums_ref[...] = sums


def join_kernel(place_ref, own_ref, beside_ref, cross_ref, corner_ref, out_ref, all_ref):
    core, side = place_ref[0], place_ref[4]
    all_ref[2 * core + side] = own_ref[...]
    all_ref[2 * core + 1 - side] = beside_ref[...]
    all_ref[2 - 2 * core + side] = cross_ref[...]
    all_ref[2 - 2 * core + 1 - side] = corner_ref[...]
    for c in range(2):
        for j in range(3):
            rows = [all_ref[2 * c + t // 2, 16 * j + t % 2 * 8 : 16 * j + t % 2 * 8 + 8] for t in range(4)]
            for m in range(2):
                out_ref[6 * c + 2 * j + m] = jnp.concatenate([row[:, 64 * m : 64 * m + 64] for row in rows], axis=1)


IN_VMEM = pl.BlockSpec(memory_space=pltpu.VMEM)
ANYWHERE = pl.BlockSpec(memory_space=pl.ANY)
IN_SMEM = pl.BlockSpec(memory_space=pltpu.SMEM)


def call(kernel, shapes, args, flops, scratch=(), special=None, out_special=None, vmem=12):
    specs = [IN_VMEM] * len(args)
    for place, spec in (special or {}).items():
        specs[place] = spec
    many = isinstance(shapes, list)
    outs = [IN_VMEM] * (len(shapes) if many else 1)
    for place, spec in (out_special or {}).items():
        outs[place] = spec
    return pl.pallas_call(
        kernel,
        out_shape=shapes,
        in_specs=specs,
        out_specs=outs if many else outs[0],
        scratch_shapes=scratch,
        compiler_params=pltpu.CompilerParams(vmem_limit_bytes=vmem * 2**20),
        cost_estimate=pl.CostEstimate(flops=flops, bytes_accessed=2**16, transcendentals=0),
    )(*args)


def per_device(queries, codes, positives, codebook):
    swap = functools.partial(lax.ppermute, axis_name="core", perm=[(0, 1), (1, 0)])
    swap_x = functools.partial(lax.ppermute, axis_name="xl", perm=[(0, 1), (1, 0)])
    shape = jax.ShapeDtypeStruct
    own_codes = codes[0]
    subspaces, passage_count = own_codes.shape
    size, width = queries.shape[1:]
    chips = 16
    half = chips * size
    offset = lax.axis_index(("xl", "z", "core")) * passage_count
    axes = [lax.axis_index(name) for name in ("core", "xh", "y", "xl")]
    place = jnp.stack([axes[0], offset, *axes[1:]]).astype(i32)
    scalar = {0: IN_SMEM}
    length = width // LANES * size + 16
    own = call(
        spread_kernel,
        shape((chips, length, LANES), bf16),
        (queries[0], positives),
        10**6,
        scratch=[pltpu.VMEM((length, LANES), bf16), pltpu.SemaphoreType.DMA((chips,))],
        out_special={0: ANYWHERE},
        vmem=60,
    )
    share = call(
        share_kernel,
        shape((codebook.shape[0] // 2, *codebook.shape[1:]), bf16),
        (place, codebook),
        10**6,
        special=scalar,
    )
    near = [share] + [lax.ppermute(share, "y", [(i, (i + k) % 4) for i in range(4)]) for k in range(1, 4)]
    near = jnp.stack(near)
    far = lax.ppermute(near, "xh", [(0, 1), (1, 0)])
    own = lax.all_to_all(own, CHIP, 0, 0)
    passages = call(
        decode_kernel,
        shape((width, passage_count), bf16),
        (place, own_codes, near, swap(near), far, swap(far)),
        10**6,
        special=scalar,
    )
    own, passages = lax.optimization_barrier((own, passages))
    other = swap(own)
    own_logs = call(own_scores_kernel, shape((4, LANES), f32), (own, passages), 10**6)
    stats = call(other_scores_kernel, shape((32, 8, LANES), f32), (other, passages, own_logs), 10**6)
    stats = lax.all_to_all(stats, CHIP + ("core",), 0, 0, tiled=True)
    query_other, query_own, grads = call(
        weights_kernel,
        [shape((half, width), f32), shape((half, width), f32), shape((width, passage_count), bf16)],
        (place, stats, own, other, passages),
        10**6,
        scratch=[
            pltpu.VMEM((2 * half, passage_count), bf16),
            pltpu.VMEM((2 * half, passage_count), bf16),
            pltpu.VMEM((width, 2 * half), bf16),
        ],
        special=scalar,
        vmem=20,
    )
    query_cross = swap(query_other)

    sums_shape = shape((8, 2, subspaces // 32, 16, LANES), f32)
    parts_cross = swap(call(codeword_kernel, sums_shape, (place, grads, own_codes), 10**6, special=scalar))
    parts, words = call(
        send_kernel,
        [sums_shape, shape((chips // 2, length, LANES), i16)],
        (place, grads, own_codes, query_own, query_cross),
        10**6,
        special=scalar,
    )
    parts = parts + parts_cross
    parts, words = lax.optimization_barrier((parts, words))
    words = swap_x(words)
    parts = lax.all_to_all(parts.reshape(16, subspaces // 32, 16, LANES), SUB + ("xl",), 0, 0)
    count = subspaces // 32 * 16
    words = call(
        pack_kernel,
        shape((chips // 2, length + count, LANES), i16),
        (place, query_own, query_cross, words, parts),
        10**6,
        special=scalar,
    )
    words = lax.all_to_all(words, "z", 0, 0)
    sums = call(functools.partial(unpack_sums_kernel, size), shape((count, LANES), f32), (words,), 10**6)
    beside = swap_x(sums)
    corner = lax.ppermute(sums, ("xl", "core"), [(i, 3 - i) for i in range(4)])
    cross = swap(sums)
    query_grad = call(unpack_query_kernel, shape((size, width), bf16), (words,), 10**6)
    codeword_grad = call(
        join_kernel,
        shape((subspaces // 8, 8, 2 * LANES), f32),
        (place, sums, beside, cross, corner),
        10**6,
        scratch=[pltpu.VMEM((4, count, LANES), f32)],
        special=scalar,
    )
    return query_grad[None], codeword_grad


def solution(mesh):
    split = Mesh(mesh.devices.reshape(2, 8, 2, 2, 4), ("xl", "z", "core", "xh", "y"))
    blk = ("xl", "z", "core")
    return jax.shard_map(
        per_device,
        mesh=split,
        in_specs=(P(SUB, blk, None), P(SUB, None, blk), P(SUB, blk), P(SUB, None, None)),
        out_specs=(P(SUB, blk, None), P(SUB, None, None)),
        check_vma=False,
    )
```

```python
import functools

import jax
import jax.numpy as jnp
from jax import lax
from jax.experimental import pallas as pl
from jax.experimental.pallas import tpu as pltpu
from jax.sharding import Mesh, PartitionSpec as P

f32 = jnp.float32
bf16 = jnp.bfloat16
i32 = jnp.int32
i16 = jnp.int16
LANES = 128
BLOCK = 256
CHIP = ("xl", "z")
SUB = ("xh", "y")
ROWS_BY_ROWS = (((1,), (1,)), ((), ()))


def exponents(rows):
    peak = jnp.maximum(jnp.max(jnp.abs(rows), axis=1, keepdims=True), 2.0**-100)
    return jnp.ceil(jnp.log2(peak * (1.0 / 32767.0)))


def as_words(rows, exponent):
    scaled = jnp.round(rows * jnp.exp2(-exponent))
    return jnp.clip(scaled, -32767.0, 32767.0).astype(i32).astype(i16)


def exponent_tails(query, sums=None):
    size = query[0].shape[0]
    lane = lax.broadcasted_iota(i32, (size, LANES), 1)
    block = jnp.zeros((size, LANES), f32)
    for c, exponent in enumerate(query):
        block = jnp.where(lane == c, exponent, block)
    parts = [block] if sums is None else [block, jnp.broadcast_to(sums, (sums.shape[0], LANES))]
    parts.append(jnp.zeros((LANES - sum(part.shape[0] for part in parts), LANES), f32))
    turned = jnp.transpose(jnp.concatenate(parts, axis=0))
    return [jnp.broadcast_to(turned[c : c + 1], (16, LANES)).astype(i32).astype(i16) for c in range(len(query))]


def scale_columns(words_ref):
    peers, length, _ = words_ref.shape
    rows = [words_ref[c, length - 16 :].astype(i32).astype(f32)[:1] for c in range(peers)]
    rows.append(jnp.zeros((LANES - peers, LANES), f32))
    return jnp.exp2(jnp.transpose(jnp.concatenate(rows, axis=0)))


def spread_kernel(queries_ref, positives_ref, out_ref, block_ref, sems):
    size, width = queries_ref.shape
    target = jnp.concatenate([positives_ref[...], jnp.zeros((1, LANES - size), i32)], axis=1)
    tail = jnp.concatenate([target // LANES, target % LANES, jnp.zeros((14, LANES), i32)], axis=0)
    for t in range(width // LANES):
        block_ref[t * size : (t + 1) * size] = queries_ref[:, t * LANES : (t + 1) * LANES]
    block_ref[width // LANES * size :] = tail.astype(f32).astype(bf16)
    sends = [pltpu.make_async_copy(block_ref, out_ref.at[c], sems.at[c]) for c in range(out_ref.shape[0])]
    for send in sends:
        send.start()
    for send in sends:
        send.wait()


def share_kernel(place_ref, book_ref, share_ref):
    count = share_ref.shape[0]
    share_ref[...] = book_ref[pl.ds(place_ref[0] * count, count)]


def query_columns(pack_ref, t, first, count):
    size = (pack_ref.shape[1] - 16) // 6
    return pack_ref[first : first + count, t * size : (t + 1) * size, :].reshape(count * size, LANES)


def query_rows(pack_ref, first, count):
    return jnp.concatenate([query_columns(pack_ref, t, first, count) for t in range(6)], axis=1)


def target_columns(packs):
    parts = []
    for pack_ref in packs:
        length = pack_ref.shape[1]
        tail = pack_ref[:, length - 16 :, :].astype(f32)
        parts.append(tail[:, 0, :] * LANES + tail[:, 1, :])
    parts.append(jnp.zeros((LANES - sum(part.shape[0] for part in parts), LANES), f32))
    return jnp.transpose(jnp.concatenate(parts, axis=0))


def decode_kernel(place_ref, codes_ref, near_ref, near_cross_ref, far_ref, far_cross_ref, out_ref):
    core, far_side, along = place_ref[0], 1 - place_ref[2], place_ref[3]
    share = near_ref.shape[1]

    def pair(j, carry):
        side, group, c, k = j // (4 * share), j // share % 4, j // (share // 2) % 2, j % (share // 2) * 2
        piece = (along + 4 - group) % 4
        rows = []
        for h in range(2):
            near = jnp.where(core == c, near_ref[piece, k + h].astype(f32), near_cross_ref[piece, k + h].astype(f32))
            far = jnp.where(core == c, far_ref[piece, k + h].astype(f32), far_cross_ref[piece, k + h].astype(f32))
            table = jnp.where(side == far_side, far, near)
            low, high = table[:, :LANES], table[:, LANES:]
            row = codes_ref[pl.ds(2 * j + h, 1), :]
            parts = []
            for t in range(row.shape[1] // LANES):
                code = jnp.broadcast_to(row[:, t * LANES : (t + 1) * LANES], (8, LANES))
                index = code & (LANES - 1)
                parts.append(
                    jnp.where(
                        code < LANES,
                        jnp.take_along_axis(low, index, axis=1, mode="promise_in_bounds"),
                        jnp.take_along_axis(high, index, axis=1, mode="promise_in_bounds"),
                    )
                )
            rows.append(jnp.concatenate(parts, axis=1))
        out_ref[pl.ds(pl.multiple_of(16 * j, 16), 16), :] = jnp.concatenate(rows, axis=0).astype(bf16)
        return carry

    lax.fori_loop(0, codes_ref.shape[0] // 2, pair, 0, unroll=8)


def local_logs(pack_ref, passages_ref):
    lane = lax.broadcasted_iota(i32, (LANES, LANES), 1)
    block = jnp.zeros((LANES, LANES), f32)
    for b in range(2):
        tile = jnp.dot(query_rows(pack_ref, b * 8, 8), passages_ref[...], preferred_element_type=f32)
        peak = jnp.max(tile, axis=1, keepdims=True)
        logs = peak + jnp.log(jnp.sum(jnp.exp(tile - peak), axis=1, keepdims=True))
        for j in range(2):
            block = jnp.where(lane == 2 * b + j, logs[j * LANES : (j + 1) * LANES], block)
    return jnp.transpose(block)[:4]


def own_scores_kernel(pack_ref, passages_ref, logs_ref):
    logs_ref[...] = local_logs(pack_ref, passages_ref)


def other_scores_kernel(pack_ref, passages_ref, own_logs_ref, stats_ref):
    logs = jnp.concatenate([own_logs_ref[...], local_logs(pack_ref, passages_ref)], axis=0)
    stats_ref[...] = jnp.broadcast_to(logs[None], stats_ref.shape)


def log_totals(core, stats_ref, h):
    peers = stats_ref.shape[0]
    same = (lax.broadcasted_iota(i32, (peers, LANES), 0) & 1) == core
    out = []
    for j in range(4):
        logs = jnp.where(same, stats_ref[:, 4 * h + j, :], stats_ref[:, 4 - 4 * h + j, :])
        peak = jnp.max(logs, axis=0, keepdims=True)
        out.append(peak + jnp.log(jnp.sum(jnp.exp(logs - peak), axis=0, keepdims=True)))
    return out


def weights_kernel(
    place_ref, stats_ref, own_ref, other_ref, passages_ref, other_sums_ref, own_sums_ref, grads_ref,
    high_ref, low_ref, turned_ref
):
    core, offset = place_ref[0], place_ref[1]
    half, passage_count = own_sums_ref.shape[0], passages_ref.shape[1]
    size = half // own_ref.shape[0]
    passages = passages_ref[...]
    spot = lax.broadcasted_iota(i32, (size, passage_count), 1) + offset
    targets = target_columns((own_ref, other_ref))[:size].astype(i32)
    logs = log_totals(core, stats_ref, 0) + log_totals(core, stats_ref, 1)
    all_totals = jnp.transpose(jnp.concatenate([*logs, jnp.zeros((LANES - 8, LANES), f32)], axis=0))
    for h, pack_ref, sums_ref in ((1, other_ref, other_sums_ref), (0, own_ref, own_sums_ref)):
        for t in range(turned_ref.shape[0] // LANES):
            columns = query_columns(pack_ref, t, 0, pack_ref.shape[0])
            turned_ref[t * LANES : (t + 1) * LANES, h * half : (h + 1) * half] = jnp.transpose(columns)
        totals = [all_totals[:, 4 * h + j : 4 * h + j + 1] for j in range(4)]
        for b in range(half // BLOCK):
            tile = jnp.dot(query_rows(pack_ref, b * 8, 8), passages, preferred_element_type=f32)
            tile = jnp.exp(tile - jnp.concatenate(totals[2 * b : 2 * b + 2], axis=0))
            rows = slice(h * half + b * BLOCK, h * half + (b + 1) * BLOCK)
            pieces = []
            for c in range(BLOCK // size):
                place = (h * half + b * BLOCK) // size + c
                hits = jnp.where(targets[:, place : place + 1] == spot, 1.0, 0.0)
                pieces.append(tile[c * size : (c + 1) * size] - hits)
            weight = jnp.concatenate(pieces, axis=0)
            high = weight.astype(bf16)
            low = (weight - high.astype(f32)).astype(bf16)
            high_ref[rows] = high
            low_ref[rows] = low
            sums_ref[b * BLOCK : (b + 1) * BLOCK] = lax.dot_general(
                high, passages, ROWS_BY_ROWS, preferred_element_type=f32
            ) + lax.dot_general(low, passages, ROWS_BY_ROWS, preferred_element_type=f32)
    for n in range(passage_count // BLOCK):
        columns = slice(n * BLOCK, (n + 1) * BLOCK)
        grad = jnp.dot(turned_ref[...], high_ref[:, columns], preferred_element_type=f32) + jnp.dot(
            turned_ref[...], low_ref[:, columns], preferred_element_type=f32
        )
        grads_ref[:, columns] = grad.astype(bf16)


def codeword_sums(core, grads_ref, codes_ref, out_ref):
    word = lax.broadcasted_iota(i32, (64, codes_ref.shape[1]), 0)

    def two(j, carry):
        first = j // 3 * 12 + 6 * core + 2 * (j % 3)
        grads = grads_ref[pl.ds(pl.multiple_of(8 * first, 16), 16), :].astype(f32)
        sums = []
        for m in range(2):
            grad = grads[8 * m : 8 * m + 8]
            code = codes_ref[pl.ds(first + m, 1), :]
            high = code >> 6
            parts = jnp.concatenate([jnp.where(high == t, grad, 0.0) for t in range(4)], axis=0).astype(bf16)
            onehot = jnp.where((code & 63) == word, 1.0, 0.0).astype(bf16)
            sums.append(lax.dot_general(parts, onehot, ROWS_BY_ROWS, preferred_element_type=f32))
        sums = jnp.concatenate(sums, axis=1)
        for k in range(2):
            out_ref[j // 3, k, j % 3] = sums[16 * k : 16 * k + 16]
        return carry

    lax.fori_loop(0, codes_ref.shape[0] // 4, two, 0, unroll=24)


def codeword_kernel(place_ref, grads_ref, codes_ref, out_ref):
    codeword_sums(1 - place_ref[0], grads_ref, codes_ref, out_ref)


def put_query_words(chunk, out_ref, c):
    size, width = chunk.shape
    exponent = exponents(chunk)
    words = as_words(chunk, exponent)
    for t in range(width // LANES):
        out_ref[c, t * size : (t + 1) * size] = words[:, t * LANES : (t + 1) * LANES]
    return exponent


def take_query_words(words_ref, c, scale, width):
    size = scale.shape[0]
    words = [words_ref[c, t * size : (t + 1) * size] for t in range(width // LANES)]
    return jnp.concatenate([word.astype(i32).astype(f32) * scale for word in words], axis=1)


def send_kernel(place_ref, grads_ref, codes_ref, sums_ref, cross_ref, parts_ref, out_ref):
    peers = out_ref.shape[0]
    half, width = sums_ref.shape
    size = half // (2 * peers)
    query = []
    for c in range(peers):
        rows = pl.ds(pl.multiple_of((1 - place_ref[4]) * (half // 2) + c * size, size), size)
        query.append(put_query_words(sums_ref[rows] + cross_ref[rows], out_ref, c))
    for c, tail in enumerate(exponent_tails(query)):
        out_ref[c, width // LANES * size :] = tail
    codeword_sums(place_ref[0], grads_ref, codes_ref, parts_ref)


def pack_kernel(place_ref, sums_ref, cross_ref, words_ref, parts_ref, out_ref):
    peers = out_ref.shape[0]
    half, width = sums_ref.shape
    size = half // (2 * peers)
    base = width // LANES * size
    totals = parts_ref[0]
    for c in range(1, parts_ref.shape[0]):
        totals = totals + parts_ref[c]
    totals = totals.reshape(-1, LANES)
    totals_exponent = exponents(totals)
    totals = as_words(totals, totals_exponent)
    scales = scale_columns(words_ref)
    query = []
    for c in range(peers):
        rows = pl.ds(pl.multiple_of(place_ref[4] * (half // 2) + c * size, size), size)
        received = take_query_words(words_ref, c, scales[:size, c : c + 1], width)
        query.append(put_query_words(sums_ref[rows] + cross_ref[rows] + received, out_ref, c))
        out_ref[c, base : base + totals.shape[0]] = totals
    for c, tail in enumerate(exponent_tails(query, totals_exponent)):
        out_ref[c, base + totals.shape[0] :] = tail


def unpack_query_kernel(words_ref, query_ref):
    peers = words_ref.shape[0]
    size, width = query_ref.shape
    scales = scale_columns(words_ref)
    query = 0.0
    for c in range(peers):
        query = query + take_query_words(words_ref, c, scales[:size, c : c + 1], width)
    query_ref[...] = query.astype(bf16)


def unpack_sums_kernel(size, words_ref, sums_ref):
    peers, length, _ = words_ref.shape
    count = sums_ref.shape[0]
    start = length - 16 - count
    scales = scale_columns(words_ref)
    sums = 0.0
    for c in range(peers):
        scale = scales[size : size + count, c : c + 1]
        sums = sums + words_ref[c, start : start + count].astype(i32).astype(f32) * scale
    sums_ref[...] = sums


def join_kernel(place_ref, own_ref, beside_ref, cross_ref, corner_ref, out_ref, all_ref):
    core, side = place_ref[0], place_ref[4]
    all_ref[2 * core + side] = own_ref[...]
    all_ref[2 * core + 1 - side] = beside_ref[...]
    all_ref[2 - 2 * core + side] = cross_ref[...]
    all_ref[2 - 2 * core + 1 - side] = corner_ref[...]
    for c in range(2):
        for j in range(3):
            rows = [all_ref[2 * c + t // 2, 16 * j + t % 2 * 8 : 16 * j + t % 2 * 8 + 8] for t in range(4)]
            for m in range(2):
                out_ref[6 * c + 2 * j + m] = jnp.concatenate([row[:, 64 * m : 64 * m + 64] for row in rows], axis=1)


IN_VMEM = pl.BlockSpec(memory_space=pltpu.VMEM)
ANYWHERE = pl.BlockSpec(memory_space=pl.ANY)
IN_SMEM = pl.BlockSpec(memory_space=pltpu.SMEM)


def call(kernel, shapes, args, flops, scratch=(), special=None, out_special=None, vmem=12):
    specs = [IN_VMEM] * len(args)
    for place, spec in (special or {}).items():
        specs[place] = spec
    many = isinstance(shapes, list)
    outs = [IN_VMEM] * (len(shapes) if many else 1)
    for place, spec in (out_special or {}).items():
        outs[place] = spec
    return pl.pallas_call(
        kernel,
        out_shape=shapes,
        in_specs=specs,
        out_specs=outs if many else outs[0],
        scratch_shapes=scratch,
        compiler_params=pltpu.CompilerParams(vmem_limit_bytes=vmem * 2**20),
        cost_estimate=pl.CostEstimate(flops=flops, bytes_accessed=2**16, transcendentals=0),
    )(*args)


def per_device(queries, codes, positives, codebook):
    swap = functools.partial(lax.ppermute, axis_name="core", perm=[(0, 1), (1, 0)])
    swap_x = functools.partial(lax.ppermute, axis_name="xl", perm=[(0, 1), (1, 0)])
    shape = jax.ShapeDtypeStruct
    own_codes = codes[0]
    subspaces, passage_count = own_codes.shape
    size, width = queries.shape[1:]
    chips = 16
    half = chips * size
    offset = lax.axis_index(("xl", "z", "core")) * passage_count
    axes = [lax.axis_index(name) for name in ("core", "xh", "y", "xl")]
    place = jnp.stack([axes[0], offset, *axes[1:]]).astype(i32)
    scalar = {0: IN_SMEM}
    length = width // LANES * size + 16
    own = call(
        spread_kernel,
        shape((chips, length, LANES), bf16),
        (queries[0], positives),
        10**6,
        scratch=[pltpu.VMEM((length, LANES), bf16), pltpu.SemaphoreType.DMA((chips,))],
        out_special={0: ANYWHERE},
        vmem=12,
    )
    share = call(
        share_kernel,
        shape((codebook.shape[0] // 2, *codebook.shape[1:]), bf16),
        (place, codebook),
        10**6,
        special=scalar,
    )
    near = [share] + [lax.ppermute(share, "y", [(i, (i + k) % 4) for i in range(4)]) for k in range(1, 4)]
    near = jnp.stack(near)
    far = lax.ppermute(near, "xh", [(0, 1), (1, 0)])
    own = lax.all_to_all(own, CHIP, 0, 0)
    passages = call(
        decode_kernel,
        shape((width, passage_count), bf16),
        (place, own_codes, near, swap(near), far, swap(far)),
        10**6,
        special=scalar,
    )
    own, passages = lax.optimization_barrier((own, passages))
    other = swap(own)
    own_logs = call(own_scores_kernel, shape((4, LANES), f32), (own, passages), 10**6)
    stats = call(other_scores_kernel, shape((32, 8, LANES), f32), (other, passages, own_logs), 10**6)
    stats = lax.all_to_all(stats, CHIP + ("core",), 0, 0, tiled=True)
    query_other, query_own, grads = call(
        weights_kernel,
        [shape((half, width), f32), shape((half, width), f32), shape((width, passage_count), bf16)],
        (place, stats, own, other, passages),
        10**6,
        scratch=[
            pltpu.VMEM((2 * half, passage_count), bf16),
            pltpu.VMEM((2 * half, passage_count), bf16),
            pltpu.VMEM((width, 2 * half), bf16),
        ],
        special=scalar,
        vmem=20,
    )
    query_cross = swap(query_other)

    sums_shape = shape((8, 2, subspaces // 32, 16, LANES), f32)
    parts_cross = swap(call(codeword_kernel, sums_shape, (place, grads, own_codes), 10**6, special=scalar))
    parts, words = call(
        send_kernel,
        [sums_shape, shape((chips // 2, length, LANES), i16)],
        (place, grads, own_codes, query_own, query_cross),
        10**6,
        special=scalar,
    )
    parts = parts + parts_cross
    parts, words = lax.optimization_barrier((parts, words))
    words = swap_x(words)
    parts = lax.all_to_all(parts.reshape(16, subspaces // 32, 16, LANES), SUB + ("xl",), 0, 0)
    count = subspaces // 32 * 16
    words = call(
        pack_kernel,
        shape((chips // 2, length + count, LANES), i16),
        (place, query_own, query_cross, words, parts),
        10**6,
        special=scalar,
    )
    words = lax.all_to_all(words, "z", 0, 0)
    sums = call(functools.partial(unpack_sums_kernel, size), shape((count, LANES), f32), (words,), 10**6)
    beside = swap_x(sums)
    corner = lax.ppermute(sums, ("xl", "core"), [(i, 3 - i) for i in range(4)])
    cross = swap(sums)
    query_grad = call(unpack_query_kernel, shape((size, width), bf16), (words,), 10**6)
    codeword_grad = call(
        join_kernel,
        shape((subspaces // 8, 8, 2 * LANES), f32),
        (place, sums, beside, cross, corner),
        10**6,
        scratch=[pltpu.VMEM((4, count, LANES), f32)],
        special=scalar,
    )
    return query_grad[None], codeword_grad


def solution(mesh):
    split = Mesh(mesh.devices.reshape(2, 8, 2, 2, 4), ("xl", "z", "core", "xh", "y"))
    blk = ("xl", "z", "core")
    return jax.shard_map(
        per_device,
        mesh=split,
        in_specs=(P(SUB, blk, None), P(SUB, None, blk), P(SUB, blk), P(SUB, None, None)),
        out_specs=(P(SUB, blk, None), P(SUB, None, None)),
        check_vma=False,
    )
```
